256 devices in a mesh: pa: 16 (over z_hi, y, core), pb: 16 (over x, z_lo).
Axes of the slice: x: 4, y: 4, z: 8 (z_hi: 2, z_lo: 4; z = z_hi * 4 + z_lo), core: 2. Of those that a mesh axis runs over, the one named last changes fastest.
Arguments:
- field: float32 [16, 64, 256, 256], P(None, 'pa', 'pb'), may hold values from -600 to 600
- spline_index: int32 [16, 64, 256, 256], P(None, 'pa', 'pb'), may hold values from 0 to 4
- spec_weight: float32 [2, 16, 16, 32, 32, 16], P(None, None, None, None, 'pa', 'pb'), may hold values from -6 to 6
- local_weight: float32 [16, 16], replicated, may hold values from -1.5 to 1.5
- bn_gain: float32 [16], replicated, may hold values from 0.1 to 1.9
- bn_shift: float32 [16], replicated, may hold values from -3 to 3
- base_weight: float32 [16, 16], replicated, may hold values from -1.5 to 1.5
- spline_coef: float32 [16, 16, 8], replicated, may hold values from -0.75 to 0.75
Outputs:
- output: float32 [16, 64, 256, 256], P(None, 'pa', 'pb')
The draws below stay inside these ranges and needn't reach their ends.
All inputs are finite; a program needn't handle non-finite values.
Results may differ from the reference program's by a relative error of at most 0.0003.
Values sent between devices are 32-bit elements; how exact they have to be, the bound alone decides.
No kernel may reach another device: no remote copies, remote signals or barrier semaphores. Data moves between devices by JAX's collectives and lax.ppermute only.
A program may use at most 128 MiB of HBM per device.

```python
import math
import jax
import jax.numpy as jnp
from jax import lax

C = 16
NZ = 64
NX = 256
NY = 256
MZ = 16
MX = 16
MY = 16
INTERVALS = 5
KZ = 32
KX = 32
NB = 8


def draw_field(key, part):
    key = jax.random.fold_in(key, 7)
    noise_key, channel_key = jax.random.split(key)
    depth = lax.broadcasted_iota(jnp.float32, (1, NZ, NX, 1), 1) / NZ
    across = lax.broadcasted_iota(jnp.float32, (1, NZ, NX, 1), 2) / NX
    channel = jnp.exp(jax.random.uniform(channel_key, (C, 1, 1, 1), jnp.float32) * math.log(10.0))
    noise = jax.random.truncated_normal(noise_key, -4.0, 4.0, (C, NZ, NX, NY), jnp.float32)
    spread = jnp.exp((depth + across) * math.log(3.0))
    return channel * (spread * noise + 0.5 * (depth + across))


def touch_ends(result, stream_key, smallest, top_value):
    longest = result.shape.index(max(result.shape))
    spots = []
    for shift in (0, 1):
        where = [jax.random.randint(jax.random.fold_in(stream_key, axis), (), 0, length) for axis, length in enumerate(result.shape)]
        where[longest] = (where[longest] + shift) % result.shape[longest]
        spots.append(tuple(where))
    return result.at[spots[0]].set(smallest).at[spots[1]].set(top_value)


def levels(rng, dims, shards, smallest, high):
    def one(position, parts):
        heights = jax.random.uniform(jax.random.fold_in(jax.random.fold_in(rng, 6), position), (parts,), jnp.float32, smallest / len(shards), high / len(shards))
        return jnp.repeat(jnp.exp(heights), dims[position] // parts).reshape((-1,) + (1,) * (len(dims) - position - 1))

    gain = one(*shards[0])
    for cut in shards[1:]:
        gain = gain * one(*cut)
    return gain


def gaussian(rng, shape, width, limit, cuts=(), held_as=jnp.bfloat16):
    entries = width * jax.random.normal(rng, shape, jnp.float32)
    if cuts:
        entries = entries * levels(rng, shape, cuts, -0.22, 0.18)
    return jnp.clip(entries, -limit, limit).astype(held_as)


def setup_inputs(seed: int = 0) -> dict:
    key_of = jax.random.split(jax.random.key(seed), 9)
    field = draw_field(jax.random.fold_in(key_of[8], 71), 0)
    spline_index = touch_ends(jax.random.randint(key_of[1], (C, NZ, NX, NY), 0, INTERVALS), jax.random.fold_in(key_of[1], 1), 0, INTERVALS - 1).astype(jnp.int32)
    spec_weight = gaussian(key_of[2], (2, C, C, KZ, KX, MY), 1.0, 6.0, ((4, 16), (5, 16)), jnp.float32)
    local_weight = gaussian(key_of[3], (C, C), C ** -0.5, 1.5, (), jnp.float32)
    bn_gain = jnp.clip(1.0 + 0.18 * jax.random.normal(key_of[4], (C,), jnp.float32), 0.1, 1.9)
    bn_shift = gaussian(key_of[5], (C,), 0.5, 3.0, (), jnp.float32)
    base_weight = gaussian(key_of[6], (C, C), C ** -0.5, 1.5, (), jnp.float32)
    spline_coef = gaussian(key_of[7], (C, C, NB), (4 * C) ** -0.5, 0.75, (), jnp.float32)
    return dict(field=field, spline_index=spline_index, spec_weight=spec_weight, local_weight=local_weight, bn_gain=bn_gain, bn_shift=bn_shift, base_weight=base_weight, spline_coef=spline_coef)


EPSILON = 1e-05
GRID_RADIUS = 2.0
HIGH = lax.Precision.HIGHEST

def spline_bases(normed, spline_index):
    step = 2.0 * GRID_RADIUS / INTERVALS
    left = spline_index.astype(normed.dtype) * step - GRID_RADIUS
    local_coord = jnp.clip((normed - left) / step, 0.0, 1.0)
    complement = 1.0 - local_coord
    cube = local_coord * local_coord * local_coord
    square = local_coord * local_coord
    pieces = [complement * complement * complement / 6.0, (3.0 * cube - 6.0 * square + 4.0) / 6.0, (-3.0 * cube + 3.0 * square + 3.0 * local_coord + 1.0) / 6.0, cube / 6.0]
    zeros = jnp.zeros_like(normed)
    columns = []
    for basis in range(NB):
        total = zeros
        for offset in range(4):
            total = total + jnp.where(spline_index == basis - offset, pieces[offset], zeros)
        columns.append(total)
    return jnp.stack(columns, axis=1)

def kan_apply(normed, spline_index, base_weight, spline_coef):
    bases = spline_bases(normed, spline_index)
    first = jnp.einsum('oi,i...->o...', base_weight, jax.nn.silu(normed), precision=HIGH)
    second = jnp.einsum('oib,ib...->o...', spline_coef, bases, precision=HIGH)
    return first + second

def corners(values, axis, count):
    lower = lax.slice_in_dim(values, 0, count, axis=axis)
    upper = lax.slice_in_dim(values, values.shape[axis] - count, values.shape[axis], axis=axis)
    return jnp.concatenate([lower, upper], axis=axis)

def reference(field, spline_index, spec_weight, local_weight, bn_gain, bn_shift, base_weight, spline_coef):
    spectrum = jnp.fft.rfftn(field, axes=(1, 2, 3))
    kept = spectrum[:, :, :, :MY]
    kept = corners(kept, 2, MX)
    kept = corners(kept, 1, MZ)
    weight = spec_weight[0] + 1j * spec_weight[1]
    mixed = jnp.einsum('iozxy,izxy->ozxy', weight, kept, precision=HIGH)
    full = jnp.zeros((C, NZ, NX, NY // 2 + 1), mixed.dtype)
    full = full.at[:, :MZ, :MX, :MY].set(mixed[:, :MZ, :MX])
    full = full.at[:, :MZ, NX - MX:, :MY].set(mixed[:, :MZ, MX:])
    full = full.at[:, NZ - MZ:, :MX, :MY].set(mixed[:, MZ:, :MX])
    full = full.at[:, NZ - MZ:, NX - MX:, :MY].set(mixed[:, MZ:, MX:])
    spectral = jnp.fft.irfftn(full, s=(NZ, NX, NY), axes=(1, 2, 3)).astype(field.dtype)
    hidden = spectral + jnp.einsum('oi,izxy->ozxy', local_weight, field, precision=HIGH)
    mean = lax.optimization_barrier(jnp.mean(hidden, axis=(1, 2, 3), keepdims=True))
    centered = hidden - mean
    var = lax.optimization_barrier(jnp.mean(centered * centered, axis=(1, 2, 3), keepdims=True))
    normed = centered * (bn_gain[:, None, None, None] * lax.rsqrt(var + EPSILON)) + bn_shift[:, None, None, None]

    def per_slab(pair):
        return kan_apply(pair[0], pair[1], base_weight, spline_coef)
    slabs = lax.map(per_slab, (jnp.moveaxis(normed, 1, 0), jnp.moveaxis(spline_index, 1, 0)))
    return jnp.moveaxis(slabs, 0, 1)
```

```python
import jax
import jax.numpy as jnp
import numpy as np
from jax import lax
from jax.experimental import pallas as pl
from jax.experimental.pallas import tpu as pltpu
from jax.sharding import PartitionSpec as P

NZ, NX, NY = 64, 256, 256
CELLS = NZ * NX * NY
BLOCK_CELLS = 4 * 16 * 256
EPSILON = 1e-05
EXACT = lax.Precision.HIGHEST
F32 = jnp.float32
B16 = jnp.bfloat16
BOTH = ("pa", "pb")
VMEM_LIMIT = 56 * 1024 * 1024

KX = np.array([[2 * p + k if p < 8 else 2 * p + k - 32 for k in range(2)] for p in range(16)])
KZ = np.array([j if j < 16 else j - 32 for j in range(32)])
KY = np.arange(16)


def split_table(table):
    high = jnp.asarray(table, F32).astype(B16)
    high = np.asarray(table, np.float32).astype(jnp.bfloat16)
    low = (np.asarray(table, np.float64) - high.astype(np.float64)).astype(jnp.bfloat16)
    return high, low


def rotation(angle, sign):
    cosine, sine = np.cos(angle), np.sin(angle)
    return np.stack([np.stack([cosine, -sign * sine]), np.stack([sign * sine, cosine])])


def tables():
    same_ky = np.eye(16)
    same_x = np.eye(4)
    angle = 2 * np.pi * (np.arange(NY)[:, None] * KY % NY) / NY
    y_part = np.stack([np.cos(angle), -np.sin(angle)], axis=1)
    y_forward = np.einsum("jJ,ypk->jyJpk", same_x, y_part).reshape(4, NY, 128)
    weight = np.where(KY == 0, 1.0, 2.0) / CELLS
    y_back = np.einsum("jJ,ypk,k->jJpky", same_x, y_part, weight).reshape(4, 128, NY)
    angle = 2 * np.pi * (KX[:, :, None] * np.arange(16) % NX) / NX
    turn = rotation(angle, -1.0)
    x_forward = np.einsum("qpahx,kK->qhakxpK", turn, same_ky).reshape(1024, 512)
    turn = rotation(angle, 1.0)
    x_back = np.einsum("qpahx,kK->phakxqK", turn, same_ky).reshape(2, 512, 512)
    z = 4 * np.arange(16)[None, :] + np.arange(4)[:, None]
    parts = []
    for frequencies in (KZ, -KZ):
        angle = 2 * np.pi * (z[:, :, None] * frequencies % NZ) / NZ
        parts.append(np.einsum("qpzaj,hH->pzhaqHj", rotation(angle, -1.0), np.eye(2)).reshape(256, 128))
    z_forward = np.concatenate(parts, axis=1)
    angle = 2 * np.pi * (z[:, :, None] * KZ % NZ) / NZ
    z_back = np.einsum("qpzaj->qzapj", rotation(angle, 1.0)).reshape(128, 64)
    return y_forward, y_back, x_forward, x_back, z_forward, z_back


Y_FORWARD, Y_BACK, X_FORWARD, X_BACK, Z_FORWARD, Z_BACK = tables()
PHASE = np.stack([np.cos(2 * np.pi * np.arange(16) / 16), np.sin(2 * np.pi * np.arange(16) / 16)]).astype(np.float32)


def split(values):
    high = values.astype(B16)
    return high, (values - high.astype(F32)).astype(B16)


def dot(left, right):
    return jnp.dot(left, right, preferred_element_type=F32)


def dot_nt(left, right, precision=None):
    return lax.dot_general(left, right, (((1,), (1,)), ((), ())), precision=precision, preferred_element_type=F32)


def dot_exact(left, right):
    return jnp.dot(left, right, precision=EXACT, preferred_element_type=F32)


def iota(shape, axis):
    return lax.broadcasted_iota(jnp.int32, shape, axis)


def phase_index(kxp, kxl, block):
    return (((2 * kxp + kxl) % 16) * block) % 16


def forward_kernel(
    ids_ref, phase_ref, left_ref, right_ref, weight_ref, y_ref, x_high_ref, x_low_ref, out_ref, sent_ref, half_ref, rows_ref
):
    pa, pb = ids_ref[0], ids_ref[1]
    rows_ref[:, 0:32] = weight_ref[...]
    wanted = jnp.where(pa < 8, 1, 0)
    chosen = rows_ref[pl.ds(wanted, 512, stride=2), :]
    sent_ref[...] = jnp.concatenate([chosen[128 * q : 128 * (q + 1), 0:32] for q in range(4)], axis=1)
    total = jnp.zeros((256, 128), F32)
    for xj in range(4):
        piece = jnp.concatenate(
            [left_ref[pl.ds(xj, 256, stride=4), :], right_ref[pl.ds(xj, 256, stride=4), :]], axis=1
        )
        high, low = split(piece)
        product = dot(high, y_ref[xj])
        total = total + product[:, 0:128] + product[:, 128:256] + dot(low, y_ref[xj, :, 0:128])
    half_ref[...] = total
    lines = jnp.concatenate(
        [
            jnp.concatenate([half_ref[pl.ds(z * 4 + x4, 16, stride=16), :] for z in range(4)], axis=0)
            for x4 in range(4)
        ],
        axis=1,
    )
    high, low = split(lines)
    first = dot_nt(x_high_ref[...], jnp.concatenate([high, low], axis=0))
    rows = first[:, 0:64] + first[:, 64:128] + dot_nt(x_low_ref[...], high)
    rows = jnp.concatenate([rows[0:512], rows[512:1024]], axis=1)
    turned = pltpu.roll(rows, 64, axis=1)
    sign = jnp.where(iota((16, 128), 1) < 64, 1.0, -1.0).astype(F32)
    for kxl in range(2):
        for kxp in range(16):
            index = phase_index(kxp, kxl, pb)
            start = (kxl * 16 + kxp) * 16
            value = (
                rows[start : start + 16] * phase_ref[0, index]
                + turned[start : start + 16] * (sign * phase_ref[1, index])
            )
            out_ref[pl.ds(kxp * 32 + kxl, 16, stride=2), :] = value


def local_kernel(
    left_ref, right_ref, index_ref, index2_ref, map_ref, base_ref, coef_ref,
    hidden_ref, level_ref, stat_ref, kan_ref, shift_ref,
):
    high, low = split(map_ref[...])
    zero = jnp.zeros((16, 16), B16)
    maps = jnp.concatenate(
        [jnp.concatenate([high, high], axis=1), jnp.concatenate([low, zero], axis=1)], axis=0
    )

    def step(x, total):
        sides = []
        for z in range(4):
            rows = pl.ds(z * 16 + x, 16, stride=64)
            high, low = split(jnp.concatenate([left_ref[rows, :], right_ref[rows, :]], axis=1))
            both = dot(maps, jnp.concatenate([high, low], axis=0))
            value = both[0:16] + both[16:32]
            total = total + value
            start = pl.multiple_of(x * 64 + z * 16, 16)
            hidden_ref[pl.ds(start, 16), :] = value
            level_ref[pl.ds(start, 16), :] = jnp.concatenate(
                [index_ref[rows, :], index2_ref[rows, :]], axis=1
            ).astype(F32)
        return total

    total = lax.fori_loop(0, 16, step, jnp.zeros((16, 256), F32))
    mean = jnp.sum(total, axis=1, keepdims=True) * (1.0 / BLOCK_CELLS)

    def spread(part, total):
        for z in range(4):
            start = pl.multiple_of(part * 64 + z * 16, 16)
            away = hidden_ref[pl.ds(start, 16), :] - mean
            total = total + away * away
        return total

    total = lax.fori_loop(0, 16, spread, jnp.zeros((16, 256), F32))
    squares = jnp.sum(total, axis=1, keepdims=True)
    first = iota((16, 128), 1) == 0
    stat_ref[0:16, :] = jnp.where(first, mean, 0.0)
    stat_ref[16:32, :] = jnp.where(first, squares, 0.0)
    last = coef_ref[:, 7, :]
    pieces = [coef_ref[:, basis, :] - last for basis in range(7)] + [base_ref[...]]
    high, low = split(jnp.concatenate(pieces, axis=1))
    kan_ref[0:16, 0:128] = high
    kan_ref[0:16, 128:256] = high
    kan_ref[16:32, 0:128] = low
    kan_ref[16:32, 128:256] = jnp.zeros((16, 128), B16)
    shift_ref[...] = jnp.broadcast_to(jnp.sum(last, axis=1, keepdims=True), (16, 128))


def mix_kernel(
    ids_ref, phase_ref, got_ref, weight_ref, partner_ref, map_ref, stat_ref, z_ref, back_ref, out_ref, rows_ref
):
    pa, pb = ids_ref[0], ids_ref[1]
    total = jnp.sum(got_ref[...].reshape(16, 4, 8, 128), axis=1)
    total = total + pltpu.roll(total, 4, axis=1)
    total = total + pltpu.roll(total, 2, axis=1)
    rows_ref[...] = total.reshape(128, 128)
    lines = jnp.concatenate([rows_ref[pl.ds(0, 16, stride=8), :], rows_ref[pl.ds(1, 16, stride=8), :]], axis=0)
    lines = lines.T
    lines = jnp.concatenate([lines[16 * q : 16 * (q + 1)] for q in range(8)], axis=1)
    modes = dot_exact(lines, z_ref[...])
    real = [modes[:, 32 * k : 32 * k + 32] for k in range(2)]
    imag = [modes[:, 64 + 32 * k : 96 + 32 * k] for k in range(2)]
    lower = pa < 8
    far_real = jnp.where(lower, modes[:, 128:160], modes[:, 160:192])
    far_imag = jnp.where(lower, modes[:, 192:224], modes[:, 224:256])
    odd = iota((32, 32), 0) % 2 == 1
    twice = (iota((32, 16), 0) // 2 == iota((32, 16), 1)).astype(F32)
    map_rows = dot_exact(twice, map_ref[...])
    mixed_real = jnp.zeros((32, 32), F32)
    mixed_imag = jnp.zeros((32, 32), F32)
    local_real = jnp.zeros((32, 32), F32)
    local_imag = jnp.zeros((32, 32), F32)
    partner_real = jnp.zeros((16, 32), F32)
    partner_imag = jnp.zeros((16, 32), F32)
    for i in range(16):
        mode_real = jnp.where(odd, real[1][i : i + 1], real[0][i : i + 1])
        mode_imag = jnp.where(odd, imag[1][i : i + 1], imag[0][i : i + 1])
        weight_real = weight_ref[32 * i : 32 * i + 32, :]
        weight_imag = weight_ref[512 + 32 * i : 544 + 32 * i, :]
        mixed_real = mixed_real + weight_real * mode_real - weight_imag * mode_imag
        mixed_imag = mixed_imag + weight_real * mode_imag + weight_imag * mode_real
        column = map_rows[:, i : i + 1]
        local_real = local_real + column * mode_real
        local_imag = local_imag + column * mode_imag
        row = 16 * (i % 8)
        lane = 32 * (i // 8)
        weight_real = partner_ref[row : row + 16, lane : lane + 32]
        weight_imag = partner_ref[row : row + 16, 64 + lane : 96 + lane]
        mode_real = far_real[i : i + 1]
        mode_imag = far_imag[i : i + 1]
        partner_real = partner_real + weight_real * mode_real + weight_imag * mode_imag
        partner_imag = partner_imag + weight_imag * mode_real - weight_real * mode_imag
    origin = jnp.logical_and(
        jnp.logical_and(pa == 0, pb == 0), jnp.logical_and(iota((32, 32), 0) % 2 == 0, iota((32, 32), 1) == 0)
    )
    centre = jnp.where(origin, mixed_real, 0.0)
    moved_real = jnp.where(origin, 0.0, mixed_real)
    moved_imag = jnp.where(origin, 0.0, mixed_imag)
    own = jnp.where(pb == 0, 0.5, 2.0)
    cross = jnp.where(pb == 0, 2.0, 4.0)
    power = own * (moved_real * moved_real + moved_imag * moved_imag)
    power = power + cross * (moved_real * local_real + moved_imag * local_imag)
    chosen = jnp.where(lower, 0, 1)
    pick = (iota((16, 32), 1) == 2 * iota((16, 32), 0) + chosen).astype(F32)
    picked = dot_exact(pick, jnp.concatenate([moved_real, moved_imag], axis=1))
    source, target = iota((32, 32), 0), iota((32, 32), 1)
    turned = jnp.logical_and(target != 16, source == (32 - target) % 32).astype(F32)
    near = dot_exact(jnp.concatenate([picked[:, 0:32], picked[:, 32:64]], axis=0), turned)
    partner_real = jnp.where(pa == 0, picked[:, 0:32], partner_real)
    partner_imag = jnp.where(pa == 0, picked[:, 32:64], partner_imag)
    pair = jnp.where(pb == 0, jnp.where(pa == 0, 0.5, 1.0), 0.0) * (
        near[0:16] * partner_real - near[16:32] * partner_imag
    )
    sums = jnp.concatenate(
        [
            power * (1.0 / CELLS),
            pair * (1.0 / CELLS),
            stat_ref[:, 0:32],
            centre * (1.0 / CELLS),
            jnp.zeros((16, 32), F32),
        ],
        axis=0,
    )
    sums = dot_nt(jnp.ones((8, 32), F32), sums, EXACT)
    out_ref[pl.ds(2, 256, stride=3), :] = jnp.broadcast_to(sums[0:1], (256, 128))
    order = (iota((32, 32), 1) == 2 * (iota((32, 32), 0) % 16) + iota((32, 32), 0) // 16).astype(F32)
    mixed = dot_exact(order, jnp.concatenate([mixed_real, mixed_imag], axis=1))
    planes = dot_nt(back_ref[...], mixed, EXACT)
    sign = jnp.where(iota((16, 128), 1) < 64, -1.0, 1.0).astype(F32)
    for kxl in range(2):
        value = jnp.concatenate(
            [planes[16 * q : 16 * (q + 1), 16 * kxl : 16 * kxl + 16] for q in range(8)], axis=1
        )
        other = pltpu.roll(value, 64, axis=1) * sign
        for block in range(16):
            index = phase_index(pa, kxl, block)
            out_ref[pl.ds(block * 3 + kxl, 16, stride=48), :] = (
                value * phase_ref[0, index] + other * phase_ref[1, index]
            )


def column(row):
    eye = (iota((16, 16), 0) == iota((16, 16), 1)).astype(F32)
    return dot_nt(eye, jnp.broadcast_to(row, (8, 16)), EXACT)[:, 0:1]


def output_kernel(
    got_ref, hidden_ref, level_ref, kan_ref, constant_ref, gain_ref, bias_ref,
    x_high_ref, x_low_ref, y_high_ref, y_low_ref, out_ref, spec_ref, result_ref, sems,
):
    stats = got_ref[pl.ds(2, 256, stride=3), :]
    sums = jnp.sum(stats, axis=0, keepdims=True)
    mean = sums * (1.0 / 256)
    away = stats - mean
    between = jnp.sum(away * away, axis=0, keepdims=True) * float(BLOCK_CELLS)
    lane = iota((1, 128), 1)
    is_mean = jnp.logical_and(lane >= 48, lane < 64)
    is_centre = jnp.logical_and(lane >= 80, lane < 112)
    variance = jnp.where(is_mean, between, jnp.where(lane < 80, sums, 0.0)) * (1.0 / CELLS)
    mean = jnp.where(is_mean, mean, jnp.where(is_centre, sums, 0.0))
    lane, row = iota((16, 128), 1), iota((16, 128), 0)
    owner = jnp.where(
        lane < 32, lane // 2, jnp.where(lane < 80, lane % 16, jnp.where(lane < 112, (lane - 80) // 2, -1))
    )
    pick = (owner == row).astype(F32)
    mean = dot_nt(pick, jnp.broadcast_to(mean, (8, 128)), EXACT)[:, 0:1]
    variance = dot_nt(pick, jnp.broadcast_to(variance, (8, 128)), EXACT)[:, 0:1]
    scale = column(gain_ref[...]) * lax.rsqrt(variance + EPSILON)
    mean = jnp.broadcast_to(jnp.concatenate([mean] * 4, axis=0), (64, 128))
    scale = jnp.broadcast_to(jnp.concatenate([scale] * 4, axis=0), (64, 128))
    bias = jnp.broadcast_to(jnp.concatenate([column(bias_ref[...])] * 4, axis=0), (64, 128))
    lines = jnp.concatenate(
        [
            got_ref[pl.ds(kxl + 384 * half, 128, stride=3), :].T
            for kxl in range(2)
            for half in range(2)
        ],
        axis=1,
    )
    high, low = split(lines)
    total = jnp.zeros((64, 512), F32)
    for part in range(2):
        rows = slice(64 * part, 64 * part + 64)
        both = dot(jnp.concatenate([high[rows], low[rows]], axis=0), x_high_ref[part])
        total = total + both[0:64] + both[64:128] + dot(high[rows], x_low_ref[part])
    lines = jnp.concatenate([total[:, 128 * x4 : 128 * (x4 + 1)] for x4 in range(4)], axis=0)
    high, low = split(lines)
    both = jnp.concatenate([high, low], axis=0)
    for xj in range(4):
        product = dot(both, y_high_ref[xj])
        value = product[0:256] + product[256:512] + dot(high, y_low_ref[xj])
        for x4 in range(4):
            start = (4 * x4 + xj) * 64
            spec_ref[start : start + 64, :] = value[64 * x4 : 64 * x4 + 64]
    weights = kan_ref[...]
    constant = constant_ref[...]
    copies = []
    for half in range(2):
        lanes = slice(128 * half, 128 * half + 128)

        def step(x, carry, half=half, lanes=lanes):
            rows = pl.ds(pl.multiple_of(x * 64, 64), 64)
            hidden = spec_ref[rows, lanes] + hidden_ref[rows, lanes]
            normed = (hidden - mean) * scale + bias
            level = level_ref[rows, lanes]
            local = jnp.clip(normed * 1.25 + (2.5 - level), 0.0, 1.0)
            other = 1.0 - local
            square = local * local
            cube = square * local
            p0 = other * other * other * (1.0 / 6.0)
            p3 = cube * (1.0 / 6.0)
            p1 = 0.5 * cube - square + 2.0 / 3.0
            p2 = 0.5 * (square + local - cube) + 1.0 / 6.0
            at = [level == float(k) for k in range(5)]
            zero = jnp.zeros_like(p0)
            pieces = [p0, p1, p2, p3]
            features = []
            for basis in range(7):
                value = zero
                for r in range(4):
                    if 0 <= basis - r <= 4:
                        value = jnp.where(at[basis - r], pieces[r], value)
                features.append(value)
            features.append(0.5 * normed * (1.0 + jnp.tanh(0.5 * normed)))
            parts = [split(value) for value in features]
            columns = []
            for z in range(4):
                columns.append(
                    jnp.concatenate(
                        [part[0][16 * z : 16 * z + 16] for part in parts]
                        + [part[1][16 * z : 16 * z + 16] for part in parts],
                        axis=0,
                    )
                )
            product = dot(weights, jnp.concatenate(columns, axis=1))
            for z in range(4):
                value = product[0:16, 128 * z : 128 * z + 128] + product[16:32, 128 * z : 128 * z + 128]
                result_ref[half, pl.ds(z * 16 + x, 16, stride=64), :] = value + constant
            return carry

        lax.fori_loop(0, 16, step, 0)
        copy = pltpu.make_async_copy(result_ref.at[half], out_ref.at[:, lanes], sems.at[half])
        copy.start()
        copies.append(copy)
    for copy in copies:
        copy.wait()


def whole():
    return pl.BlockSpec(memory_space=pltpu.VMEM)


def scalars():
    return pl.BlockSpec(memory_space=pltpu.SMEM)


def sides(rows):
    return [pl.BlockSpec((rows, 128), lambda step, h=h: (0, h)) for h in range(2)]


def params():
    return pltpu.CompilerParams(vmem_limit_bytes=VMEM_LIMIT)


def cost(flops, moved):
    return pl.CostEstimate(flops=flops, bytes_accessed=moved, transcendentals=0)


def shape(dims, dtype=F32):
    return jax.ShapeDtypeStruct(dims, dtype)


def on_device(
    field, spline_index, spec_weight, local_weight, bn_gain, bn_shift, base_weight, spline_coef
):
    ids = jnp.stack([lax.axis_index("pa"), lax.axis_index("pb")]).astype(jnp.int32)
    phase = jnp.asarray(PHASE)
    field = field.reshape(1024, 256)
    index = spline_index.reshape(1024, 256)
    weight = jnp.transpose(spec_weight, (0, 1, 2, 4, 5, 3)).reshape(1024, 32)
    y_high, y_low = split_table(Y_FORWARD)
    x_high, x_low = split_table(X_FORWARD)
    sent, own = pl.pallas_call(
        forward_kernel,
        grid=(1,),
        out_shape=(shape((512, 128)), shape((128, 128))),
        in_specs=[scalars(), scalars(), *sides(1024)] + [whole()] * 4,
        out_specs=(whole(), whole()),
        scratch_shapes=[pltpu.VMEM((256, 128), F32), pltpu.VMEM((1024, 128), F32)],
        compiler_params=params(),
        cost_estimate=cost(4 * 10**8, 4 * 10**6),
        name="forward",
    )(
        ids, phase, field, field, weight,
        jnp.asarray(np.concatenate([y_high, y_low], axis=2)), jnp.asarray(x_high), jnp.asarray(x_low),
    )
    path = [0]
    while path[-1] != 8:
        path.append(15 - path[-1] if path[-1] < 8 else 16 - path[-1])
    partner = lax.ppermute(own, BOTH, [(16 * a, 16 * b) for a, b in zip(path[:-1], path[1:])])
    got = lax.all_to_all(sent.reshape(256, 2, 128), BOTH, 0, 0, tiled=True).reshape(512, 128)
    hidden, level, stat, kan, constant = pl.pallas_call(
        local_kernel,
        grid=(1,),
        out_shape=(
            shape((1024, 256)), shape((1024, 256)), shape((32, 128)), shape((32, 256), B16), shape((16, 128)),
        ),
        in_specs=sides(1024) + sides(1024) + [whole()] * 3,
        out_specs=(whole(),) * 5,
        compiler_params=params(),
        cost_estimate=cost(10**8, 4 * 10**6),
        name="local",
    )(field, field, index, index, local_weight, base_weight, jnp.transpose(spline_coef, (0, 2, 1)))
    back = pl.pallas_call(
        mix_kernel,
        out_shape=shape((768, 128)),
        in_specs=[scalars(), scalars()] + [whole()] * 7,
        out_specs=whole(),
        scratch_shapes=[pltpu.VMEM((128, 128), F32)],
        compiler_params=params(),
        cost_estimate=cost(10**7, 10**6),
        name="mix",
    )(
        ids, phase, got, weight, partner, local_weight, stat,
        jnp.asarray(Z_FORWARD, F32), jnp.asarray(Z_BACK, F32),
    )
    back = lax.all_to_all(back.reshape(256, 3, 128), BOTH, 0, 0, tiled=True).reshape(768, 128)
    x_high, x_low = split_table(X_BACK)
    y_high, y_low = split_table(Y_BACK)
    output = pl.pallas_call(
        output_kernel,
        out_shape=shape((1024, 256)),
        in_specs=[whole()] * 11,
        out_specs=pl.BlockSpec(memory_space=pl.ANY),
        scratch_shapes=[
            pltpu.VMEM((1024, 256), F32),
            pltpu.VMEM((2, 1024, 128), F32),
            pltpu.SemaphoreType.DMA((2,)),
        ],
        compiler_params=params(),
        cost_estimate=cost(10**9, 6 * 10**6),
        name="output",
    )(
        back, hidden, level, kan, constant, bn_gain.reshape(1, 16), bn_shift.reshape(1, 16),
        jnp.asarray(x_high), jnp.asarray(x_low), jnp.asarray(y_high), jnp.asarray(y_low),
    )
    return output.reshape(16, 4, 16, 256)


def solution(mesh):
    in_specs = (
        P(None, "pa", "pb", None),
        P(None, "pa", "pb", None),
        P(None, None, None, None, "pa", "pb"),
        P(),
        P(),
        P(),
        P(),
        P(),
    )
    out_specs = P(None, "pa", "pb", None)
    return jax.shard_map(
        on_device, mesh=mesh, in_specs=in_specs, out_specs=out_specs, check_vma=False
    )
```

```python
import jax
import jax.numpy as jnp
import numpy as np
from jax import lax
from jax.experimental import pallas as pl
from jax.experimental.pallas import tpu as pltpu
from jax.sharding import PartitionSpec as P

NZ, NX, NY = 64, 256, 256
CELLS = NZ * NX * NY
BLOCK_CELLS = 4 * 16 * 256
EPSILON = 1e-05
EXACT = lax.Precision.HIGHEST
F32 = jnp.float32
B16 = jnp.bfloat16
BOTH = ("pa", "pb")
MIB = 1024 * 1024

KZ = np.array([j if j < 16 else j - 32 for j in range(32)])
KY = np.arange(16)


def split_table(table):
    high = jnp.asarray(table, F32).astype(B16)
    high = np.asarray(table, np.float32).astype(jnp.bfloat16)
    low = (np.asarray(table, np.float64) - high.astype(np.float64)).astype(jnp.bfloat16)
    return high, low


def rotation(angle, sign):
    cosine, sine = np.cos(angle), np.sin(angle)
    return np.stack([np.stack([cosine, -sign * sine]), np.stack([sign * sine, cosine])])


def tables():
    same_x = np.eye(4)
    angle = 2 * np.pi * (np.arange(NY)[:, None] * KY % NY) / NY
    y_part = np.stack([np.cos(angle), -np.sin(angle)], axis=1)
    y_forward = np.einsum("jJ,ypk->jyJpk", same_x, y_part).reshape(4, NY, 128)
    weight = np.where(KY == 0, 1.0, 2.0) / CELLS
    y_back = np.einsum("jJ,ypk,k->jpJky", same_x, y_part, weight).reshape(4, 128, NY)
    z = 4 * np.arange(16)[None, :] + np.arange(4)[:, None]
    angle = 2 * np.pi * (z[:, :, None] * KZ % NZ) / NZ
    z_forward = np.einsum("qpzaj,hH->pzhaqHj", rotation(angle, -1.0), np.eye(2)).reshape(256, 128)
    angle = 2 * np.pi * (z[:, :, None] * KZ % NZ) / NZ
    z_back = np.einsum("qpzaj->qzapj", rotation(angle, 1.0)).reshape(128, 64)
    return y_forward, y_back, z_forward, z_back


Y_FORWARD, Y_BACK, Z_FORWARD, Z_BACK = tables()
PHASE = np.stack([np.cos(2 * np.pi * np.arange(512) / 512), np.sin(2 * np.pi * np.arange(512) / 512)]).astype(np.float32)


def split(values):
    high = values.astype(B16)
    return high, (values - high.astype(F32)).astype(B16)


def dot(left, right):
    return jnp.dot(left, right, preferred_element_type=F32)


def dot_nt(left, right, precision=None):
    return lax.dot_general(left, right, (((1,), (1,)), ((), ())), precision=precision, preferred_element_type=F32)


def dot_exact(left, right):
    return jnp.dot(left, right, precision=EXACT, preferred_element_type=F32)


def iota(shape, axis):
    return lax.broadcasted_iota(jnp.int32, shape, axis)


def phase_index(frequency, block):
    return (frequency * (32 * block + 15)) & 511


def place(frequency):
    return (frequency % 32) // 2, frequency % 2


def cosine(frequency, step):
    return float(np.cos(2 * np.pi * frequency * (step + 0.5) / NX))


def sine(frequency, step):
    return float(np.sin(2 * np.pi * frequency * (step + 0.5) / NX))


def signs(rows, first):
    return jnp.where(iota((rows, 128), 1) < 64, first, -first).astype(F32)


def forward_kernel(
    phase_hbm, field_hbm, weight_hbm, y_hbm, out_ref, sent_ref, kept_ref,
    phase_ref, half_ref, rows_ref, field_ref, weight_ref, y_ref, sems,
):
    pa, pb = lax.axis_index("pa"), lax.axis_index("pb")
    copies = [
        pltpu.make_async_copy(source, target, sems.at[number])
        for number, (source, target) in enumerate(
            [
                (field_hbm.at[:, 0:128], field_ref.at[0]),
                (field_hbm.at[:, 128:256], field_ref.at[1]),
                (y_hbm, y_ref),
                (weight_hbm, weight_ref),
                (phase_hbm, phase_ref),
            ]
        )
    ]
    for copy in copies:
        copy.start()
    for copy in copies[0:3]:
        copy.wait()
    total = jnp.zeros((256, 128), F32)
    for xj in range(4):
        piece = jnp.concatenate(
            [field_ref[half, pl.ds(xj, 256, stride=4), :] for half in range(2)], axis=1
        )
        high, low = split(piece)
        product = dot(high, y_ref[xj])
        total = total + product[:, 0:128] + product[:, 128:256] + dot(low, y_ref[xj, :, 0:128])
    half_ref[...] = total
    copies[4].wait()
    lines = []
    for x4 in range(4):
        piece = jnp.concatenate([half_ref[pl.ds(z * 4 + x4, 16, stride=16), :] for z in range(4)], axis=0).T
        for xj in range(4):
            lines.append(jnp.concatenate([piece[32 * xj : 32 * xj + 16], piece[32 * xj + 16 : 32 * xj + 32]], axis=1))
    sign = signs(8, 1.0)
    for half in range(2):
        rows = slice(8 * half, 8 * half + 8)
        even = [lines[8 + j][rows] + lines[7 - j][rows] for j in range(8)]
        odd = [pltpu.roll(lines[8 + j][rows] - lines[7 - j][rows], 64, axis=1) * sign for j in range(8)]
        for frequency in range(17):
            first = sum(even[j] * cosine(frequency, j) for j in range(8))
            second = sum(odd[j] * sine(frequency, j) for j in range(8))
            values = {}
            if frequency < 16:
                values[frequency] = first + second
            if frequency > 0:
                values[-frequency] = first - second
            for signed, value in values.items():
                index = phase_index(signed, pb)
                kxp, kxl = place(signed)
                out_ref[pl.ds(kxp * 32 + kxl + 16 * half, 8, stride=2), :] = value * phase_ref[0, index] + pltpu.roll(
                    value, 64, axis=1
                ) * (sign * phase_ref[1, index])
    copies[3].wait()
    rows_ref[:, 0:32] = weight_ref[...]
    for target, wanted in ((sent_ref, jnp.where(pa < 8, 1, 0)), (kept_ref, 0)):
        chosen = rows_ref[pl.ds(wanted, 512, stride=2), :]
        target[...] = jnp.concatenate([chosen[128 * q : 128 * (q + 1), 0:32] for q in range(4)], axis=1)


def local_kernel(
    field_hbm, map_ref, base_ref, coef_ref, hidden_hbm, stat_hbm, kan_hbm, shift_hbm,
    field_ref, hidden_ref, stat_ref, kan_ref, shift_ref, sems, out_sems,
):
    copies = [
        pltpu.make_async_copy(field_hbm.at[:, 128 * half : 128 * half + 128], field_ref.at[half], sems.at[half])
        for half in range(2)
    ]
    for copy in copies:
        copy.start()
    last = coef_ref[:, 7, :]
    pieces = [coef_ref[:, basis, :] - last for basis in range(7)] + [base_ref[...]]
    high, low = split(jnp.concatenate(pieces, axis=1))
    kan_ref[0:16, 0:128] = high
    kan_ref[0:16, 128:256] = high
    kan_ref[16:32, 0:128] = low
    kan_ref[16:32, 128:256] = jnp.zeros((16, 128), B16)
    shift_ref[...] = jnp.broadcast_to(jnp.sum(last, axis=1, keepdims=True), (16, 128))
    outs = [
        pltpu.make_async_copy(source, target, out_sems.at[number])
        for number, (source, target) in enumerate(
            [(kan_ref, kan_hbm), (shift_ref, shift_hbm), (hidden_ref, hidden_hbm), (stat_ref, stat_hbm)]
        )
    ]
    outs[0].start()
    outs[1].start()
    high, low = split(map_ref[...])
    zero = jnp.zeros((16, 16), B16)
    maps = jnp.concatenate(
        [jnp.concatenate([high, high], axis=1), jnp.concatenate([low, zero], axis=1)], axis=0
    )
    for copy in copies:
        copy.wait()

    def step(x, total):
        for z in range(4):
            rows = pl.ds(z * 16 + x, 16, stride=64)
            high, low = split(jnp.concatenate([field_ref[half, rows, :] for half in range(2)], axis=1))
            both = dot(maps, jnp.concatenate([high, low], axis=0))
            value = both[0:16] + both[16:32]
            total = total + value
            start = pl.multiple_of(x * 64 + z * 16, 16)
            hidden_ref[pl.ds(start, 16), :] = value
        return total

    total = lax.fori_loop(0, 16, step, jnp.zeros((16, 256), F32), unroll=4)
    outs[2].start()
    mean = jnp.sum(total, axis=1, keepdims=True) * (1.0 / BLOCK_CELLS)

    def spread(part, total):
        for z in range(4):
            start = pl.multiple_of(part * 64 + z * 16, 16)
            away = hidden_ref[pl.ds(start, 16), :] - mean
            total = total + away * away
        return total

    total = lax.fori_loop(0, 16, spread, jnp.zeros((16, 256), F32), unroll=4)
    squares = jnp.sum(total, axis=1, keepdims=True)
    first = iota((16, 128), 1) == 0
    stat_ref[0:16, :] = jnp.where(first, mean, 0.0)
    stat_ref[16:32, :] = jnp.where(first, squares, 0.0)
    outs[3].start()
    for copy in outs:
        copy.wait()


def mix_kernel(
    phase_hbm, got_hbm, weight_hbm, partner_hbm, kept_hbm, map_hbm, stat_hbm, z_hbm, back_hbm, out_ref,
    phase_ref, got_ref, map_ref, z_ref, back_ref, rows_ref, weight_ref, partner_ref, stat_ref, both_ref, sems,
):
    pa, pb = lax.axis_index("pa"), lax.axis_index("pb")
    copies = [
        pltpu.make_async_copy(source, target, sems.at[number])
        for number, (source, target) in enumerate(
            [
                (got_hbm, got_ref),
                (z_hbm, z_ref),
                (map_hbm, map_ref),
                (weight_hbm, weight_ref),
                (stat_hbm, stat_ref),
                (back_hbm, back_ref),
                (phase_hbm, phase_ref),
                (partner_hbm, partner_ref),
            ]
        )
    ]
    for copy in copies[0:7]:
        copy.start()

    @pl.when(pa == 0)
    def _():
        pltpu.make_async_copy(kept_hbm, partner_ref, sems.at[7]).start()

    @pl.when(pa != 0)
    def _():
        copies[7].start()

    for copy in copies[0:3]:
        copy.wait()
    total = jnp.sum(got_ref[...].reshape(16, 4, 8, 128), axis=1)
    total = total + pltpu.roll(total, 4, axis=1)
    total = total + pltpu.roll(total, 2, axis=1)
    rows_ref[...] = total.reshape(128, 128)
    lines = jnp.concatenate([rows_ref[pl.ds(0, 16, stride=8), :], rows_ref[pl.ds(1, 16, stride=8), :]], axis=0)
    lines = lines.T
    lines = jnp.concatenate([lines[16 * q : 16 * (q + 1)] for q in range(8)], axis=1)
    modes = dot_exact(lines, z_ref[...])
    real = [modes[:, 32 * k : 32 * k + 32] for k in range(2)]
    imag = [modes[:, 64 + 32 * k : 96 + 32 * k] for k in range(2)]
    lower = pa < 8
    far_real = jnp.where(lower, real[0], real[1])
    far_imag = jnp.where(lower, imag[0], imag[1])
    odd = iota((32, 32), 0) % 2 == 1
    twice = (iota((32, 16), 0) // 2 == iota((32, 16), 1)).astype(F32)
    map_rows = dot_exact(twice, map_ref[...])
    mixed_real = jnp.zeros((32, 32), F32)
    mixed_imag = jnp.zeros((32, 32), F32)
    local_real = jnp.zeros((32, 32), F32)
    local_imag = jnp.zeros((32, 32), F32)
    partner_real = jnp.zeros((32, 32), F32)
    partner_imag = jnp.zeros((32, 32), F32)
    for copy in copies[3:8]:
        copy.wait()
    source, target = iota((128, 128), 0), iota((128, 128), 1)
    turn = jnp.logical_and(source // 32 == target // 32, source % 32 == (32 - target % 32) % 32)
    turn = jnp.logical_and(turn, target % 32 != 16).astype(F32)
    turned = dot_exact(partner_ref[...], turn)
    both_ref[pl.ds(0, 128, stride=2), :] = turned
    both_ref[pl.ds(1, 128, stride=2), :] = turned
    for i in range(16):
        mode_real = jnp.where(odd, real[1][i : i + 1], real[0][i : i + 1])
        mode_imag = jnp.where(odd, imag[1][i : i + 1], imag[0][i : i + 1])
        weight_real = weight_ref[32 * i : 32 * i + 32, :]
        weight_imag = weight_ref[512 + 32 * i : 544 + 32 * i, :]
        mixed_real = mixed_real + weight_real * mode_real - weight_imag * mode_imag
        mixed_imag = mixed_imag + weight_real * mode_imag + weight_imag * mode_real
        column = map_rows[:, i : i + 1]
        local_real = local_real + column * mode_real
        local_imag = local_imag + column * mode_imag
        row = 32 * (i % 8)
        lane = 32 * (i // 8)
        weight_real = both_ref[row : row + 32, lane : lane + 32]
        weight_imag = both_ref[row : row + 32, 64 + lane : 96 + lane]
        mode_real = far_real[i : i + 1]
        mode_imag = far_imag[i : i + 1]
        partner_real = partner_real + weight_real * mode_real + weight_imag * mode_imag
        partner_imag = partner_imag + weight_imag * mode_real - weight_real * mode_imag
    origin = jnp.logical_and(
        jnp.logical_and(pa == 0, pb == 0), jnp.logical_and(iota((32, 32), 0) % 2 == 0, iota((32, 32), 1) == 0)
    )
    centre = jnp.where(origin, mixed_real, 0.0)
    moved_real = jnp.where(origin, 0.0, mixed_real)
    moved_imag = jnp.where(origin, 0.0, mixed_imag)
    own = jnp.where(pb == 0, 0.5, 2.0)
    cross = jnp.where(pb == 0, 2.0, 4.0)
    power = own * (moved_real * moved_real + moved_imag * moved_imag)
    power = power + cross * (moved_real * local_real + moved_imag * local_imag)
    pair = moved_real * partner_real - moved_imag * partner_imag
    chosen = jnp.where(lower, 0, 1)
    pair = jnp.where(
        jnp.logical_and(pb == 0, iota((32, 32), 0) % 2 == chosen), jnp.where(pa == 0, 0.5, 1.0) * pair, 0.0
    )
    power = power + pair
    sums = jnp.concatenate(
        [
            power * (1.0 / CELLS),
            jnp.zeros((16, 32), F32),
            stat_ref[:, 0:32],
            centre * (1.0 / CELLS),
            jnp.zeros((16, 32), F32),
        ],
        axis=0,
    )
    sums = dot_nt(jnp.ones((8, 32), F32), sums, EXACT)
    out_ref[pl.ds(2, 256, stride=3), :] = jnp.broadcast_to(sums[0:1], (256, 128))
    order = (iota((32, 32), 1) == 2 * (iota((32, 32), 0) % 16) + iota((32, 32), 0) // 16).astype(F32)
    mixed = dot_exact(order, jnp.concatenate([mixed_real, mixed_imag], axis=1))
    planes = dot_nt(back_ref[...], mixed, EXACT)
    sign = signs(16, -1.0)
    for kxl in range(2):
        frequency = 2 * pa + kxl - jnp.where(lower, 0, 32)
        value = jnp.concatenate(
            [planes[16 * q : 16 * (q + 1), 16 * kxl : 16 * kxl + 16] for q in range(8)], axis=1
        )
        other = pltpu.roll(value, 64, axis=1) * sign
        for block in range(16):
            index = phase_index(frequency, block)
            out_ref[pl.ds(block * 3 + kxl, 16, stride=48), :] = (
                value * phase_ref[0, index] + other * phase_ref[1, index]
            )


def column(row):
    eye = (iota((16, 16), 0) == iota((16, 16), 1)).astype(F32)
    return dot_nt(eye, jnp.broadcast_to(row, (8, 16)), EXACT)[:, 0:1]


def output_kernel(
    got_hbm, hidden_hbm, index_hbm, kan_hbm, constant_hbm, gain_hbm, bias_hbm,
    y_high_hbm, y_low_hbm, out_ref,
    gain_ref, bias_ref, got_ref, y_high_ref, y_low_ref,
    spec_ref, result_ref, hidden_ref, index_ref, kan_ref, constant_ref, in_sems, sems,
):
    reads = [
        pltpu.make_async_copy(source, target, in_sems.at[number])
        for number, (source, target) in enumerate(
            [
                (got_hbm, got_ref),
                (gain_hbm, gain_ref),
                (bias_hbm, bias_ref),
                (y_high_hbm, y_high_ref),
                (y_low_hbm, y_low_ref),
                (kan_hbm, kan_ref),
                (constant_hbm, constant_ref),
                (hidden_hbm.at[:, 0:128], hidden_ref.at[:, 0:128]),
                (index_hbm.at[:, 0:128], index_ref.at[0]),
                (hidden_hbm.at[:, 128:256], hidden_ref.at[:, 128:256]),
                (index_hbm.at[:, 128:256], index_ref.at[1]),
            ]
        )
    ]
    for copy in reads[0:5]:
        copy.start()
    for copy in reads[0:3]:
        copy.wait()
    for copy in reads[5:11]:
        copy.start()
    stats = got_ref[pl.ds(2, 256, stride=3), :]
    sums = jnp.sum(stats, axis=0, keepdims=True)
    mean = sums * (1.0 / 256)
    away = stats - mean
    between = jnp.sum(away * away, axis=0, keepdims=True) * float(BLOCK_CELLS)
    lane = iota((1, 128), 1)
    is_mean = jnp.logical_and(lane >= 48, lane < 64)
    is_centre = jnp.logical_and(lane >= 80, lane < 112)
    variance = jnp.where(is_mean, between, jnp.where(lane < 80, sums, 0.0)) * (1.0 / CELLS)
    mean = jnp.where(is_mean, mean, jnp.where(is_centre, sums, 0.0))
    lane, row = iota((16, 128), 1), iota((16, 128), 0)
    owner = jnp.where(
        lane < 32, lane // 2, jnp.where(lane < 80, lane % 16, jnp.where(lane < 112, (lane - 80) // 2, -1))
    )
    pick = (owner == row).astype(F32)
    mean = dot_nt(pick, jnp.broadcast_to(mean, (8, 128)), EXACT)[:, 0:1]
    variance = dot_nt(pick, jnp.broadcast_to(variance, (8, 128)), EXACT)[:, 0:1]
    scale = column(gain_ref[...]) * lax.rsqrt(variance + EPSILON)
    mean = jnp.broadcast_to(jnp.concatenate([mean] * 4, axis=0), (64, 128))
    scale = jnp.broadcast_to(jnp.concatenate([scale] * 4, axis=0), (64, 128))
    bias = jnp.broadcast_to(jnp.concatenate([column(bias_ref[...])] * 4, axis=0), (64, 128))
    lines = [[None] * 2 for _ in range(16)]
    sign = signs(8, -1.0)
    for half in range(2):
        modes = {}
        for frequency in range(-16, 16):
            kxp, kxl = place(frequency)
            modes[frequency] = got_ref[pl.ds(kxp * 48 + kxl + 24 * half, 8, stride=3), :]
        even = [modes[k] + modes[-k] for k in range(1, 16)] + [modes[-16]]
        odd = [modes[k] - modes[-k] for k in range(1, 16)] + [-modes[-16]]
        odd = [pltpu.roll(value, 64, axis=1) * sign for value in odd]
        for j in range(8):
            first = modes[0] + sum(even[k - 1] * cosine(k, j) for k in range(1, 17))
            second = sum(odd[k - 1] * sine(k, j) for k in range(1, 17))
            lines[8 + j][half] = first + second
            lines[7 - j][half] = first - second
    groups = []
    for x4 in range(4):
        piece = jnp.concatenate([lines[4 * x4 + xj][half] for xj in range(4) for half in range(2)], axis=0).T
        groups.append(jnp.concatenate([piece[0:64], piece[64:128]], axis=1))
    high, low = split(jnp.concatenate(groups, axis=0))
    both = jnp.concatenate([high, low], axis=0)
    reads[3].wait()
    reads[4].wait()
    for xj in range(4):
        product = dot(both, y_high_ref[xj])
        value = product[0:256] + product[256:512] + dot(high, y_low_ref[xj])
        for x4 in range(4):
            start = (4 * x4 + xj) * 64
            spec_ref[start : start + 64, :] = value[64 * x4 : 64 * x4 + 64]
    for copy in reads[5:9]:
        copy.wait()
    weights = kan_ref[...]
    constant = constant_ref[...]
    copies = []
    for half in range(2):
        lanes = slice(128 * half, 128 * half + 128)
        if half == 1:
            reads[9].wait()
            reads[10].wait()

        def step(x, carry, half=half, lanes=lanes):
            rows = pl.ds(pl.multiple_of(x * 64, 64), 64)
            hidden = spec_ref[rows, lanes] + hidden_ref[rows, lanes]
            normed = (hidden - mean) * scale + bias
            level = jnp.concatenate(
                [index_ref[half, pl.ds(z * 16 + x, 16, stride=64), :] for z in range(4)], axis=0
            ).astype(F32)
            local = jnp.clip(normed * 1.25 + (2.5 - level), 0.0, 1.0)
            other = 1.0 - local
            square = local * local
            cube = square * local
            p0 = other * other * other * (1.0 / 6.0)
            p3 = cube * (1.0 / 6.0)
            p1 = 0.5 * cube - square + 2.0 / 3.0
            p2 = 0.5 * (square + local - cube) + 1.0 / 6.0
            level = level.astype(B16)
            at = [level == jnp.asarray(k, B16) for k in range(5)]
            zero = jnp.zeros((64, 128), B16)
            pieces = [split(piece) for piece in (p0, p1, p2, p3)]
            parts = []
            for basis in range(7):
                value = [zero, zero]
                for r in range(4):
                    if 0 <= basis - r <= 4:
                        value = [jnp.where(at[basis - r], pieces[r][k], value[k]) for k in range(2)]
                parts.append(value)
            parts.append(split(0.5 * normed * (1.0 + jnp.tanh(0.5 * normed))))
            columns = []
            for z in range(4):
                columns.append(
                    jnp.concatenate(
                        [part[0][16 * z : 16 * z + 16] for part in parts]
                        + [part[1][16 * z : 16 * z + 16] for part in parts],
                        axis=0,
                    )
                )
            product = dot(weights, jnp.concatenate(columns, axis=1))
            for z in range(4):
                value = product[0:16, 128 * z : 128 * z + 128] + product[16:32, 128 * z : 128 * z + 128]
                result_ref[half, pl.ds(z * 16 + x, 16, stride=64), :] = value + constant
            return carry

        for part in range(2):
            lax.fori_loop(8 * part, 8 * part + 8, step, 0, unroll=8)
            copy = pltpu.make_async_copy(
                result_ref.at[half].reshape(64, 16, 128).at[:, 8 * part : 8 * part + 8, :],
                out_ref.at[:, 8 * part : 8 * part + 8, lanes],
                sems.at[2 * half + part],
            )
            copy.start()
            copies.append(copy)
    for copy in copies:
        copy.wait()


def whole():
    return pl.BlockSpec(memory_space=pltpu.VMEM)


def scalars():
    return pl.BlockSpec(memory_space=pltpu.SMEM)


def hbm():
    return pl.BlockSpec(memory_space=pltpu.HBM)


def params(vmem):
    return pltpu.CompilerParams(vmem_limit_bytes=vmem * MIB)


def cost(flops, moved):
    return pl.CostEstimate(flops=flops, bytes_accessed=moved, transcendentals=0)


def shape(dims, dtype=F32):
    return jax.ShapeDtypeStruct(dims, dtype)


def transfers(count):
    return pltpu.SemaphoreType.DMA((count,))


def forward_call(field, weight):
    y_high, y_low = split_table(Y_FORWARD)
    return pl.pallas_call(
        forward_kernel,
        out_shape=(shape((512, 128)), shape((128, 128)), shape((128, 128))),
        in_specs=[hbm()] * 4,
        out_specs=(whole(),) * 3,
        scratch_shapes=[
            pltpu.SMEM((2, 512), F32),
            pltpu.VMEM((256, 128), F32),
            pltpu.VMEM((1024, 128), F32),
            pltpu.VMEM((2, 1024, 128), F32),
            pltpu.VMEM((1024, 32), F32),
            pltpu.VMEM((4, 256, 256), B16),
            transfers(5),
        ],
        compiler_params=params(60),
        cost_estimate=cost(4 * 10**8, 4 * 10**6),
        name="forward",
    )(
        jnp.asarray(PHASE), field, weight,
        jnp.asarray(np.concatenate([y_high, y_low], axis=2)),
    )


def local_call(field, local_weight, base_weight, spline_coef):
    return pl.pallas_call(
        local_kernel,
        out_shape=(shape((1024, 256)), shape((32, 128)), shape((32, 256), B16), shape((16, 128))),
        in_specs=[hbm()] + [whole()] * 3,
        out_specs=(hbm(),) * 4,
        scratch_shapes=[
            pltpu.VMEM((2, 1024, 128), F32),
            pltpu.VMEM((1024, 256), F32),
            pltpu.VMEM((32, 128), F32),
            pltpu.VMEM((32, 256), B16),
            pltpu.VMEM((16, 128), F32),
            transfers(2),
            transfers(4),
        ],
        compiler_params=params(60),
        cost_estimate=cost(10**8, 2 * 10**6),
        name="local",
    )(field, local_weight, base_weight, jnp.transpose(spline_coef, (0, 2, 1)))


def mix_call(got, weight, partner, kept, local_weight, stat):
    return pl.pallas_call(
        mix_kernel,
        out_shape=shape((768, 128)),
        in_specs=[hbm()] * 9,
        out_specs=whole(),
        scratch_shapes=[
            pltpu.SMEM((2, 512), F32),
            pltpu.VMEM((512, 128), F32),
            pltpu.VMEM((16, 16), F32),
            pltpu.VMEM((256, 128), F32),
            pltpu.VMEM((128, 64), F32),
            pltpu.VMEM((128, 128), F32),
            pltpu.VMEM((1024, 32), F32),
            pltpu.VMEM((128, 128), F32),
            pltpu.VMEM((32, 128), F32),
            pltpu.VMEM((256, 128), F32),
            transfers(8),
        ],
        compiler_params=params(60),
        cost_estimate=cost(10**7, 10**6),
        name="mix",
    )(
        jnp.asarray(PHASE), got, weight, partner, kept, local_weight, stat,
        jnp.asarray(Z_FORWARD, F32), jnp.asarray(Z_BACK, F32),
    )


def output_call(back, hidden, index, kan, constant, bn_gain, bn_shift):
    y_high, y_low = split_table(Y_BACK)
    return pl.pallas_call(
        output_kernel,
        out_shape=shape((64, 16, 256)),
        in_specs=[hbm()] * 9,
        out_specs=hbm(),
        scratch_shapes=[
            pltpu.VMEM((1, 16), F32),
            pltpu.VMEM((1, 16), F32),
            pltpu.VMEM((768, 128), F32),
            pltpu.VMEM((4, 128, 256), B16),
            pltpu.VMEM((4, 128, 256), B16),
            pltpu.VMEM((1024, 256), F32),
            pltpu.VMEM((2, 1024, 128), F32),
            pltpu.VMEM((1024, 256), F32),
            pltpu.VMEM((2, 1024, 128), jnp.int32),
            pltpu.VMEM((32, 256), B16),
            pltpu.VMEM((16, 128), F32),
            transfers(11),
            transfers(4),
        ],
        compiler_params=params(60),
        cost_estimate=cost(10**9, 6 * 10**6),
        name="output",
    )(
        back, hidden, index, kan, constant, bn_gain.reshape(1, 16), bn_shift.reshape(1, 16),
        jnp.asarray(y_high), jnp.asarray(y_low),
    )


def on_device(
    field, spline_index, spec_weight, local_weight, bn_gain, bn_shift, base_weight, spline_coef
):
    field = field.reshape(1024, 256)
    index = spline_index.reshape(1024, 256)
    weight = jnp.transpose(spec_weight, (0, 1, 2, 4, 5, 3)).reshape(1024, 32)
    sent, own, kept = forward_call(field, weight)
    path = [0]
    while path[-1] != 8:
        path.append(15 - path[-1] if path[-1] < 8 else 16 - path[-1])
    partner = lax.ppermute(own, BOTH, [(16 * a, 16 * b) for a, b in zip(path[:-1], path[1:])])
    got = lax.all_to_all(sent.reshape(256, 2, 128), BOTH, 0, 0, tiled=True).reshape(512, 128)
    hidden, stat, kan, constant = local_call(field, local_weight, base_weight, spline_coef)
    back = mix_call(got, weight, partner, kept, local_weight, stat)
    back = lax.all_to_all(back.reshape(256, 1, 384), BOTH, 0, 0, tiled=True).reshape(768, 128)
    output = output_call(back, hidden, index, kan, constant, bn_gain, bn_shift)
    return output.reshape(16, 4, 16, 256)


def solution(mesh):
    in_specs = (
        P(None, "pa", "pb", None),
        P(None, "pa", "pb", None),
        P(None, None, None, None, "pa", "pb"),
        P(),
        P(),
        P(),
        P(),
        P(),
    )
    out_specs = P(None, "pa", "pb", None)
    return jax.shard_map(
        on_device, mesh=mesh, in_specs=in_specs, out_specs=out_specs, check_vma=False
    )
```

```python
import jax
import jax.numpy as jnp
import numpy as np
from jax import lax
from jax.experimental import pallas as pl
from jax.experimental.pallas import tpu as pltpu
from jax.sharding import PartitionSpec as P

NZ, NX, NY = 64, 256, 256
CELLS = NZ * NX * NY
BLOCK_CELLS = 4 * 16 * 256
EPSILON = 1e-05
EXACT = lax.Precision.HIGHEST
F32 = jnp.float32
B16 = jnp.bfloat16
BOTH = ("pa", "pb")
MIB = 1024 * 1024
PITCH = 72

KZ = np.array([j if j < 16 else j - 32 for j in range(32)])
KY = np.arange(16)


def split_table(table):
    high = jnp.asarray(table, F32).astype(B16)
    high = np.asarray(table, np.float32).astype(jnp.bfloat16)
    low = (np.asarray(table, np.float64) - high.astype(np.float64)).astype(jnp.bfloat16)
    return high, low


def rotation(angle, sign):
    cosine, sine = np.cos(angle), np.sin(angle)
    return np.stack([np.stack([cosine, -sign * sine]), np.stack([sign * sine, cosine])])


def tables():
    same_x = np.eye(4)
    angle = 2 * np.pi * (np.arange(NY)[:, None] * KY % NY) / NY
    y_part = np.stack([np.cos(angle), -np.sin(angle)], axis=1)
    y_forward = np.einsum("jJ,ypk->jyJpk", same_x, y_part).reshape(4, NY, 128)
    weight = np.where(KY == 0, 1.0, 2.0) / CELLS
    y_back = np.einsum("jJ,ypk,k->jpJky", same_x, y_part, weight).reshape(4, 128, NY)
    z = 4 * np.arange(16)[None, :] + np.arange(4)[:, None]
    angle = 2 * np.pi * (z[:, :, None] * KZ % NZ) / NZ
    z_forward = np.einsum("qpzaj,hH->pzhaqHj", rotation(angle, -1.0), np.eye(2)).reshape(256, 128)
    angle = 2 * np.pi * (z[:, :, None] * KZ % NZ) / NZ
    z_back = np.einsum("qpzaj->qzapj", rotation(angle, 1.0)).reshape(128, 64)
    return y_forward, y_back, z_forward, z_back


Y_FORWARD, Y_BACK, Z_FORWARD, Z_BACK = tables()
PHASE = np.stack([np.cos(2 * np.pi * np.arange(512) / 512), np.sin(2 * np.pi * np.arange(512) / 512)]).astype(np.float32)


def split(values):
    high = values.astype(B16)
    return high, (values - high.astype(F32)).astype(B16)


def dot(left, right):
    return jnp.dot(left, right, preferred_element_type=F32)


def dot_nt(left, right, precision=None):
    return lax.dot_general(left, right, (((1,), (1,)), ((), ())), precision=precision, preferred_element_type=F32)


def dot_exact(left, right):
    return jnp.dot(left, right, precision=EXACT, preferred_element_type=F32)


def iota(shape, axis):
    return lax.broadcasted_iota(jnp.int32, shape, axis)


def phase_index(frequency, block):
    return (frequency * (32 * block + 15)) & 511


def place(frequency):
    return (frequency % 32) // 2, frequency % 2


def cosine(frequency, step):
    return float(np.cos(2 * np.pi * frequency * (step + 0.5) / NX))


def sine(frequency, step):
    return float(np.sin(2 * np.pi * frequency * (step + 0.5) / NX))


def signs(rows, first):
    return jnp.where(iota((rows, 128), 1) < 64, first, -first).astype(F32)


def forward_kernel(
    phase_hbm, field_hbm, weight_hbm, y_hbm, out_ref, sent_ref, kept_ref,
    phase_ref, half_ref, rows_ref, field_ref, weight_ref, y_ref, sems,
):
    pa, pb = lax.axis_index("pa"), lax.axis_index("pb")
    copies = [
        pltpu.make_async_copy(source, target, sems.at[number])
        for number, (source, target) in enumerate(
            [
                (field_hbm.at[:, 0:128], field_ref.at[0]),
                (field_hbm.at[:, 128:256], field_ref.at[1]),
                (y_hbm, y_ref),
                (weight_hbm, weight_ref),
                (phase_hbm, phase_ref),
            ]
        )
    ]
    for copy in copies:
        copy.start()
    for copy in copies[0:3]:
        copy.wait()
    total = jnp.zeros((256, 128), F32)
    for xj in range(4):
        piece = jnp.concatenate(
            [field_ref[half, pl.ds(xj, 256, stride=4), :] for half in range(2)], axis=1
        )
        high, low = split(piece)
        product = dot(high, y_ref[xj])
        total = total + product[:, 0:128] + product[:, 128:256] + dot(low, y_ref[xj, :, 0:128])
    half_ref[...] = total
    copies[4].wait()
    lines = []
    for x4 in range(4):
        piece = jnp.concatenate([half_ref[pl.ds(z * 4 + x4, 16, stride=16), :] for z in range(4)], axis=0).T
        for xj in range(4):
            lines.append(jnp.concatenate([piece[32 * xj : 32 * xj + 16], piece[32 * xj + 16 : 32 * xj + 32]], axis=1))
    sign = signs(8, 1.0)
    for half in range(2):
        rows = slice(8 * half, 8 * half + 8)
        even = [lines[8 + j][rows] + lines[7 - j][rows] for j in range(8)]
        odd = [pltpu.roll(lines[8 + j][rows] - lines[7 - j][rows], 64, axis=1) * sign for j in range(8)]
        for frequency in range(17):
            first = sum(even[j] * cosine(frequency, j) for j in range(8))
            second = sum(odd[j] * sine(frequency, j) for j in range(8))
            values = {}
            if frequency < 16:
                values[frequency] = first + second
            if frequency > 0:
                values[-frequency] = first - second
            for signed, value in values.items():
                index = phase_index(signed, pb)
                kxp, kxl = place(signed)
                out_ref[pl.ds(kxp * 32 + kxl + 16 * half, 8, stride=2), :] = value * phase_ref[0, index] + pltpu.roll(
                    value, 64, axis=1
                ) * (sign * phase_ref[1, index])
    copies[3].wait()
    rows_ref[:, 0:32] = weight_ref[...]
    for target, wanted in ((sent_ref, jnp.where(pa < 8, 1, 0)), (kept_ref, 0)):
        chosen = rows_ref[pl.ds(wanted, 512, stride=2), :]
        target[...] = jnp.concatenate([chosen[128 * q : 128 * (q + 1), 0:32] for q in range(4)], axis=1)


def local_kernel(
    field_hbm, map_hbm, base_hbm, coef_hbm, hidden_hbm, stat_ref, kan_hbm, shift_hbm,
    map_ref, base_ref, coef_ref, field_ref, hidden_ref, kan_ref, shift_ref, sems, out_sems,
):
    copies = [
        pltpu.make_async_copy(
            field_hbm.at[:, :, 128 * half : 128 * half + 128],
            field_ref.at[half].reshape(16, PITCH, 128).at[:, 0:64, :],
            sems.at[half],
        )
        for half in range(2)
    ]
    small = [
        pltpu.make_async_copy(source, target, sems.at[2 + number])
        for number, (source, target) in enumerate([(map_hbm, map_ref), (base_hbm, base_ref), (coef_hbm, coef_ref)])
    ]
    for copy in small + copies:
        copy.start()
    for copy in small:
        copy.wait()
    last = coef_ref[:, 7, :]
    pieces = [coef_ref[:, basis, :] - last for basis in range(7)] + [base_ref[...]]
    high, low = split(jnp.concatenate(pieces, axis=1))
    kan_ref[0:16, 0:128] = high
    kan_ref[0:16, 128:256] = high
    kan_ref[16:32, 0:128] = low
    kan_ref[16:32, 128:256] = jnp.zeros((16, 128), B16)
    shift_ref[...] = jnp.broadcast_to(jnp.sum(last, axis=1, keepdims=True), (16, 128))
    outs = [
        pltpu.make_async_copy(source, target, out_sems.at[number])
        for number, (source, target) in enumerate(
            [(kan_ref, kan_hbm), (shift_ref, shift_hbm), (hidden_ref, hidden_hbm)]
        )
    ]
    outs[0].start()
    outs[1].start()
    high, low = split(map_ref[...])
    zero = jnp.zeros((16, 16), B16)
    maps = jnp.concatenate(
        [jnp.concatenate([high, high], axis=1), jnp.concatenate([low, zero], axis=1)], axis=0
    )
    for copy in copies:
        copy.wait()

    def step(x, total):
        for z in range(4):
            rows = pl.ds(z * 16 + x, 16, stride=PITCH)
            high, low = split(jnp.concatenate([field_ref[half, rows, :] for half in range(2)], axis=1))
            both = dot(maps, jnp.concatenate([high, low], axis=0))
            value = both[0:16] + both[16:32]
            total = total + value
            start = pl.multiple_of(x * 64 + z * 16, 16)
            hidden_ref[pl.ds(start, 16), :] = value
        return total

    total = lax.fori_loop(0, 16, step, jnp.zeros((16, 256), F32), unroll=4)
    outs[2].start()
    mean = jnp.sum(total, axis=1, keepdims=True) * (1.0 / BLOCK_CELLS)

    def spread(part, total):
        for z in range(4):
            start = pl.multiple_of(part * 64 + z * 16, 16)
            away = hidden_ref[pl.ds(start, 16), :] - mean
            total = total + away * away
        return total

    total = lax.fori_loop(0, 16, spread, jnp.zeros((16, 256), F32), unroll=4)
    squares = jnp.sum(total, axis=1, keepdims=True)
    first = iota((16, 128), 1) == 0
    stat_ref[0:16, :] = jnp.where(first, mean, 0.0)
    stat_ref[16:32, :] = jnp.where(first, squares, 0.0)
    for copy in outs:
        copy.wait()


def mix_kernel(
    got_ref, partner_ref, kept_ref, stat_ref, phase_hbm, weight_hbm, map_hbm, z_hbm, back_hbm, out_ref,
    phase_ref, map_ref, z_ref, back_ref, rows_ref, weight_ref, both_ref, sems,
):
    pa, pb = lax.axis_index("pa"), lax.axis_index("pb")
    copies = [
        pltpu.make_async_copy(source, target, sems.at[number])
        for number, (source, target) in enumerate(
            [
                (z_hbm, z_ref),
                (map_hbm, map_ref),
                (weight_hbm, weight_ref),
                (back_hbm, back_ref),
                (phase_hbm, phase_ref),
            ]
        )
    ]
    for copy in copies:
        copy.start()
    total = jnp.sum(got_ref[...].reshape(16, 4, 8, 128), axis=1)
    total = total + pltpu.roll(total, 4, axis=1)
    total = total + pltpu.roll(total, 2, axis=1)
    rows_ref[...] = total.reshape(128, 128)
    lines = jnp.concatenate([rows_ref[pl.ds(0, 16, stride=8), :], rows_ref[pl.ds(1, 16, stride=8), :]], axis=0)
    lines = lines.T
    lines = jnp.concatenate([lines[16 * q : 16 * (q + 1)] for q in range(8)], axis=1)
    for copy in copies:
        copy.wait()
    modes = dot_exact(lines, z_ref[...])
    real = [modes[:, 32 * k : 32 * k + 32] for k in range(2)]
    imag = [modes[:, 64 + 32 * k : 96 + 32 * k] for k in range(2)]
    lower = pa < 8
    far_real = jnp.where(lower, real[0], real[1])
    far_imag = jnp.where(lower, imag[0], imag[1])
    odd = iota((32, 32), 0) % 2 == 1
    twice = (iota((32, 16), 0) // 2 == iota((32, 16), 1)).astype(F32)
    map_rows = dot_exact(twice, map_ref[...])
    mixed_real = jnp.zeros((32, 32), F32)
    mixed_imag = jnp.zeros((32, 32), F32)
    local_real = jnp.zeros((32, 32), F32)
    local_imag = jnp.zeros((32, 32), F32)
    partner_real = jnp.zeros((32, 32), F32)
    partner_imag = jnp.zeros((32, 32), F32)
    source, target = iota((128, 128), 0), iota((128, 128), 1)
    turn = jnp.logical_and(source // 32 == target // 32, source % 32 == (32 - target % 32) % 32)
    turn = jnp.logical_and(turn, target % 32 != 16).astype(F32)
    turned = dot_exact(jnp.where(pa == 0, kept_ref[...], partner_ref[...]), turn)
    both_ref[pl.ds(0, 128, stride=2), :] = turned
    both_ref[pl.ds(1, 128, stride=2), :] = turned
    for i in range(16):
        mode_real = jnp.where(odd, real[1][i : i + 1], real[0][i : i + 1])
        mode_imag = jnp.where(odd, imag[1][i : i + 1], imag[0][i : i + 1])
        weight_real = weight_ref[32 * i : 32 * i + 32, :]
        weight_imag = weight_ref[512 + 32 * i : 544 + 32 * i, :]
        mixed_real = mixed_real + weight_real * mode_real - weight_imag * mode_imag
        mixed_imag = mixed_imag + weight_real * mode_imag + weight_imag * mode_real
        column = map_rows[:, i : i + 1]
        local_real = local_real + column * mode_real
        local_imag = local_imag + column * mode_imag
        row = 32 * (i % 8)
        lane = 32 * (i // 8)
        weight_real = both_ref[row : row + 32, lane : lane + 32]
        weight_imag = both_ref[row : row + 32, 64 + lane : 96 + lane]
        mode_real = far_real[i : i + 1]
        mode_imag = far_imag[i : i + 1]
        partner_real = partner_real + weight_real * mode_real + weight_imag * mode_imag
        partner_imag = partner_imag + weight_imag * mode_real - weight_real * mode_imag
    origin = jnp.logical_and(
        jnp.logical_and(pa == 0, pb == 0), jnp.logical_and(iota((32, 32), 0) % 2 == 0, iota((32, 32), 1) == 0)
    )
    centre = jnp.where(origin, mixed_real, 0.0)
    moved_real = jnp.where(origin, 0.0, mixed_real)
    moved_imag = jnp.where(origin, 0.0, mixed_imag)
    own = jnp.where(pb == 0, 0.5, 2.0)
    cross = jnp.where(pb == 0, 2.0, 4.0)
    power = own * (moved_real * moved_real + moved_imag * moved_imag)
    power = power + cross * (moved_real * local_real + moved_imag * local_imag)
    pair = moved_real * partner_real - moved_imag * partner_imag
    chosen = jnp.where(lower, 0, 1)
    pair = jnp.where(
        jnp.logical_and(pb == 0, iota((32, 32), 0) % 2 == chosen), jnp.where(pa == 0, 0.5, 1.0) * pair, 0.0
    )
    power = power + pair
    sums = jnp.concatenate(
        [
            power * (1.0 / CELLS),
            jnp.zeros((16, 32), F32),
            stat_ref[:, 0:32],
            centre * (1.0 / CELLS),
            jnp.zeros((16, 32), F32),
        ],
        axis=0,
    )
    sums = dot_nt(jnp.ones((8, 32), F32), sums, EXACT)
    out_ref[pl.ds(2, 256, stride=3), :] = jnp.broadcast_to(sums[0:1], (256, 128))
    order = (iota((32, 32), 1) == 2 * (iota((32, 32), 0) % 16) + iota((32, 32), 0) // 16).astype(F32)
    mixed = dot_exact(order, jnp.concatenate([mixed_real, mixed_imag], axis=1))
    planes = dot_nt(back_ref[...], mixed, EXACT)
    sign = signs(16, -1.0)
    for kxl in range(2):
        frequency = 2 * pa + kxl - jnp.where(lower, 0, 32)
        value = jnp.concatenate(
            [planes[16 * q : 16 * (q + 1), 16 * kxl : 16 * kxl + 16] for q in range(8)], axis=1
        )
        other = pltpu.roll(value, 64, axis=1) * sign
        for block in range(16):
            index = phase_index(frequency, block)
            out_ref[pl.ds(block * 3 + kxl, 16, stride=48), :] = (
                value * phase_ref[0, index] + other * phase_ref[1, index]
            )


def column(row):
    eye = (iota((16, 16), 0) == iota((16, 16), 1)).astype(F32)
    return dot_nt(eye, jnp.broadcast_to(row, (8, 16)), EXACT)[:, 0:1]


def output_kernel(
    got_ref, hidden_hbm, index_hbm, kan_hbm, constant_hbm, gain_hbm, bias_hbm,
    y_high_hbm, y_low_hbm, out_ref,
    gain_ref, bias_ref, y_high_ref, y_low_ref,
    spec_ref, result_ref, hidden_ref, index_ref, kan_ref, constant_ref, in_sems, sems,
):
    reads = [
        pltpu.make_async_copy(source, target, in_sems.at[number])
        for number, (source, target) in enumerate(
            [
                (gain_hbm, gain_ref),
                (bias_hbm, bias_ref),
                (y_high_hbm, y_high_ref),
                (y_low_hbm, y_low_ref),
                (kan_hbm, kan_ref),
                (constant_hbm, constant_ref),
                (hidden_hbm.at[:, 0:128], hidden_ref.at[:, 0:128]),
                (index_hbm.at[:, :, 0:128], index_ref.at[0].reshape(16, PITCH, 128).at[:, 0:64, :]),
                (hidden_hbm.at[:, 128:256], hidden_ref.at[:, 128:256]),
                (index_hbm.at[:, :, 128:256], index_ref.at[1].reshape(16, PITCH, 128).at[:, 0:64, :]),
            ]
        )
    ]
    for copy in reads:
        copy.start()
    stats = got_ref[pl.ds(2, 256, stride=3), :]
    sums = jnp.sum(stats, axis=0, keepdims=True)
    mean = sums * (1.0 / 256)
    away = stats - mean
    between = jnp.sum(away * away, axis=0, keepdims=True) * float(BLOCK_CELLS)
    lane = iota((1, 128), 1)
    is_mean = jnp.logical_and(lane >= 48, lane < 64)
    is_centre = jnp.logical_and(lane >= 80, lane < 112)
    variance = jnp.where(is_mean, between, jnp.where(lane < 80, sums, 0.0)) * (1.0 / CELLS)
    mean = jnp.where(is_mean, mean, jnp.where(is_centre, sums, 0.0))
    lane, row = iota((16, 128), 1), iota((16, 128), 0)
    owner = jnp.where(
        lane < 32, lane // 2, jnp.where(lane < 80, lane % 16, jnp.where(lane < 112, (lane - 80) // 2, -1))
    )
    pick = (owner == row).astype(F32)
    mean = dot_nt(pick, jnp.broadcast_to(mean, (8, 128)), EXACT)[:, 0:1]
    variance = dot_nt(pick, jnp.broadcast_to(variance, (8, 128)), EXACT)[:, 0:1]
    reads[0].wait()
    reads[1].wait()
    scale = column(gain_ref[...]) * lax.rsqrt(variance + EPSILON)
    mean = jnp.broadcast_to(jnp.concatenate([mean] * 4, axis=0), (64, 128))
    scale = jnp.broadcast_to(jnp.concatenate([scale] * 4, axis=0), (64, 128))
    bias = jnp.broadcast_to(jnp.concatenate([column(bias_ref[...])] * 4, axis=0), (64, 128))
    lines = [[None] * 2 for _ in range(16)]
    sign = signs(8, -1.0)
    for half in range(2):
        modes = {}
        for frequency in range(-16, 16):
            kxp, kxl = place(frequency)
            modes[frequency] = got_ref[pl.ds(kxp * 48 + kxl + 24 * half, 8, stride=3), :]
        even = [modes[k] + modes[-k] for k in range(1, 16)] + [modes[-16]]
        odd = [modes[k] - modes[-k] for k in range(1, 16)] + [-modes[-16]]
        odd = [pltpu.roll(value, 64, axis=1) * sign for value in odd]
        for j in range(8):
            first = modes[0] + sum(even[k - 1] * cosine(k, j) for k in range(1, 17))
            second = sum(odd[k - 1] * sine(k, j) for k in range(1, 17))
            lines[8 + j][half] = first + second
            lines[7 - j][half] = first - second
    groups = []
    for x4 in range(4):
        piece = jnp.concatenate([lines[4 * x4 + xj][half] for xj in range(4) for half in range(2)], axis=0).T
        groups.append(jnp.concatenate([piece[0:64], piece[64:128]], axis=1))
    high, low = split(jnp.concatenate(groups, axis=0))
    both = jnp.concatenate([high, low], axis=0)
    reads[2].wait()
    reads[3].wait()
    for xj in range(4):
        product = dot(both, y_high_ref[xj])
        value = product[0:256] + product[256:512] + dot(high, y_low_ref[xj])
        for x4 in range(4):
            start = (4 * x4 + xj) * 64
            spec_ref[start : start + 64, :] = value[64 * x4 : 64 * x4 + 64]
    for copy in reads[4:8]:
        copy.wait()
    weights = kan_ref[...]
    constant = constant_ref[...]
    copies = []
    for half in range(2):
        lanes = slice(128 * half, 128 * half + 128)
        if half == 1:
            reads[8].wait()
            reads[9].wait()

        def step(x, carry, half=half, lanes=lanes):
            rows = pl.ds(pl.multiple_of(x * 64, 64), 64)
            hidden = spec_ref[rows, lanes] + hidden_ref[rows, lanes]
            normed = (hidden - mean) * scale + bias
            level = jnp.concatenate(
                [index_ref[half, pl.ds(z * 16 + x, 16, stride=PITCH), :] for z in range(4)], axis=0
            ).astype(F32)
            local = jnp.clip(normed * 1.25 + (2.5 - level), 0.0, 1.0)
            other = 1.0 - local
            square = local * local
            cube = square * local
            p0 = other * other * other * (1.0 / 6.0)
            p3 = cube * (1.0 / 6.0)
            p1 = 0.5 * cube - square + 2.0 / 3.0
            p2 = 0.5 * (square + local - cube) + 1.0 / 6.0
            level = level.astype(B16)
            at = [level == jnp.asarray(k, B16) for k in range(5)]
            zero = jnp.zeros((64, 128), B16)
            pieces = [split(piece) for piece in (p0, p1, p2, p3)]
            parts = []
            for basis in range(7):
                value = [zero, zero]
                for r in range(4):
                    if 0 <= basis - r <= 4:
                        value = [jnp.where(at[basis - r], pieces[r][k], value[k]) for k in range(2)]
                parts.append(value)
            parts.append(split(0.5 * normed * (1.0 + jnp.tanh(0.5 * normed))))
            columns = []
            for z in range(4):
                columns.append(
                    jnp.concatenate(
                        [part[0][16 * z : 16 * z + 16] for part in parts]
                        + [part[1][16 * z : 16 * z + 16] for part in parts],
                        axis=0,
                    )
                )
            product = dot(weights, jnp.concatenate(columns, axis=1))
            for z in range(4):
                value = product[0:16, 128 * z : 128 * z + 128] + product[16:32, 128 * z : 128 * z + 128]
                result_ref[half, pl.ds(z * 16 + x, 16, stride=PITCH), :] = value + constant
            return carry

        for part in range(2):
            lax.fori_loop(8 * part, 8 * part + 8, step, 0, unroll=8)
            for z in range(4):
                row = 16 * z + 8 * part
                copy = pltpu.make_async_copy(
                    result_ref.at[half].reshape(16, PITCH, 128).at[:, row : row + 8, :],
                    out_ref.at[:, row : row + 8, lanes],
                    sems.at[8 * half + 4 * part + z],
                )
                copy.start()
                copies.append(copy)
    for copy in copies:
        copy.wait()


def whole():
    return pl.BlockSpec(memory_space=pltpu.VMEM)


def scalars():
    return pl.BlockSpec(memory_space=pltpu.SMEM)


def hbm():
    return pl.BlockSpec(memory_space=pltpu.HBM)


def params(vmem):
    return pltpu.CompilerParams(vmem_limit_bytes=vmem * MIB)


def cost(flops, moved):
    return pl.CostEstimate(flops=flops, bytes_accessed=moved, transcendentals=0)


def shape(dims, dtype=F32):
    return jax.ShapeDtypeStruct(dims, dtype)


def far(*arrays):
    return [pltpu.with_memory_space_constraint(array, pltpu.HBM) for array in arrays]


def near(*arrays):
    return [pltpu.with_memory_space_constraint(array, pltpu.VMEM) for array in arrays]


def transfers(count):
    return pltpu.SemaphoreType.DMA((count,))


def forward_call(field, weight):
    y_high, y_low = split_table(Y_FORWARD)
    return pl.pallas_call(
        forward_kernel,
        out_shape=(pltpu.VMEM((512, 128), F32), pltpu.VMEM((128, 128), F32), pltpu.VMEM((128, 128), F32)),
        in_specs=[hbm()] * 4,
        out_specs=(whole(),) * 3,
        scratch_shapes=[
            pltpu.SMEM((2, 512), F32),
            pltpu.VMEM((256, 128), F32),
            pltpu.VMEM((1024, 128), F32),
            pltpu.VMEM((2, 1024, 128), F32),
            pltpu.VMEM((1024, 32), F32),
            pltpu.VMEM((4, 256, 256), B16),
            transfers(5),
        ],
        compiler_params=params(24),
        cost_estimate=cost(4 * 10**8, 4 * 10**6),
        name="forward",
    )(
        *far(jnp.asarray(PHASE), field, weight, jnp.asarray(np.concatenate([y_high, y_low], axis=2)))
    )


def local_call(field, local_weight, base_weight, spline_coef):
    return pl.pallas_call(
        local_kernel,
        out_shape=(
            pltpu.HBM((1024, 256), F32), pltpu.VMEM((32, 128), F32), pltpu.HBM((32, 256), B16), pltpu.HBM((16, 128), F32),
        ),
        in_specs=[hbm()] * 4,
        out_specs=(hbm(), whole(), hbm(), hbm()),
        scratch_shapes=[
            pltpu.VMEM((16, 16), F32),
            pltpu.VMEM((16, 16), F32),
            pltpu.VMEM((16, 8, 16), F32),
            pltpu.VMEM((2, 16 * PITCH, 128), F32),
            pltpu.VMEM((1024, 256), F32),
            pltpu.VMEM((32, 256), B16),
            pltpu.VMEM((16, 128), F32),
            transfers(5),
            transfers(3),
        ],
        compiler_params=params(24),
        cost_estimate=cost(10**8, 2 * 10**6),
        name="local",
    )(*far(field.reshape(16, 64, 256), local_weight, base_weight, jnp.transpose(spline_coef, (0, 2, 1))))


def mix_call(got, weight, partner, kept, local_weight, stat):
    return pl.pallas_call(
        mix_kernel,
        out_shape=pltpu.VMEM((768, 128), F32),
        in_specs=[whole()] * 4 + [hbm()] * 5,
        out_specs=whole(),
        scratch_shapes=[
            pltpu.SMEM((2, 512), F32),
            pltpu.VMEM((16, 16), F32),
            pltpu.VMEM((256, 128), F32),
            pltpu.VMEM((128, 64), F32),
            pltpu.VMEM((128, 128), F32),
            pltpu.VMEM((1024, 32), F32),
            pltpu.VMEM((256, 128), F32),
            transfers(5),
        ],
        compiler_params=params(24),
        cost_estimate=cost(10**7, 10**6),
        name="mix",
    )(
        *near(got, partner, kept, stat),
        *far(jnp.asarray(PHASE), weight, local_weight, jnp.asarray(Z_FORWARD, F32), jnp.asarray(Z_BACK, F32)),
    )


def output_call(back, hidden, index, kan, constant, bn_gain, bn_shift):
    y_high, y_low = split_table(Y_BACK)
    return pl.pallas_call(
        output_kernel,
        out_shape=pltpu.HBM((16, 64, 256), F32),
        in_specs=[whole()] + [hbm()] * 8,
        out_specs=hbm(),
        scratch_shapes=[
            pltpu.VMEM((1, 16), F32),
            pltpu.VMEM((1, 16), F32),
            pltpu.VMEM((4, 128, 256), B16),
            pltpu.VMEM((4, 128, 256), B16),
            pltpu.VMEM((1024, 256), F32),
            pltpu.VMEM((2, 16 * PITCH, 128), F32),
            pltpu.VMEM((1024, 256), F32),
            pltpu.VMEM((2, 16 * PITCH, 128), jnp.int32),
            pltpu.VMEM((32, 256), B16),
            pltpu.VMEM((16, 128), F32),
            transfers(10),
            transfers(16),
        ],
        compiler_params=params(24),
        cost_estimate=cost(10**9, 6 * 10**6),
        name="output",
    )(
        *near(back),
        *far(
            hidden, index.reshape(16, 64, 256), kan, constant, bn_gain.reshape(1, 16), bn_shift.reshape(1, 16),
            jnp.asarray(y_high), jnp.asarray(y_low),
        ),
    )


def on_device(
    field, spline_index, spec_weight, local_weight, bn_gain, bn_shift, base_weight, spline_coef
):
    field = field.reshape(1024, 256)
    index = spline_index.reshape(1024, 256)
    weight = jnp.transpose(spec_weight, (0, 1, 2, 4, 5, 3)).reshape(1024, 32)
    sent, own, kept = forward_call(field, weight)
    path = [0]
    while path[-1] != 8:
        path.append(15 - path[-1] if path[-1] < 8 else 16 - path[-1])
    partner = lax.ppermute(own, BOTH, [(16 * a, 16 * b) for a, b in zip(path[:-1], path[1:])])
    got = lax.all_to_all(sent.reshape(256, 2, 128), BOTH, 0, 0, tiled=True).reshape(512, 128)
    hidden, stat, kan, constant = local_call(field, local_weight, base_weight, spline_coef)
    back = mix_call(got, weight, partner, kept, local_weight, stat)
    back = lax.all_to_all(back.reshape(256, 1, 384), BOTH, 0, 0, tiled=True).reshape(768, 128)
    output = output_call(back, hidden, index, kan, constant, bn_gain, bn_shift)
    return output.reshape(16, 4, 16, 256)


def solution(mesh):
    in_specs = (
        P(None, "pa", "pb", None),
        P(None, "pa", "pb", None),
        P(None, None, None, None, "pa", "pb"),
        P(),
        P(),
        P(),
        P(),
        P(),
    )
    out_specs = P(None, "pa", "pb", None)
    return jax.shard_map(
        on_device, mesh=mesh, in_specs=in_specs, out_specs=out_specs, check_vma=False
    )
```

```python
import jax
import jax.numpy as jnp
import numpy as np
from jax import lax
from jax.experimental import pallas as pl
from jax.experimental.pallas import tpu as pltpu
from jax.sharding import PartitionSpec as P

NZ, NX, NY = 64, 256, 256
CELLS = NZ * NX * NY
BLOCK_CELLS = 4 * 16 * 256
EPSILON = 1e-05
EXACT = lax.Precision.HIGHEST
F32 = jnp.float32
B16 = jnp.bfloat16
BOTH = ("pa", "pb")
MIB = 1024 * 1024
PITCH = 72

KZ = np.array([j if j < 16 else j - 32 for j in range(32)])
KY = np.arange(16)


def split_table(table):
    high = jnp.asarray(table, F32).astype(B16)
    high = np.asarray(table, np.float32).astype(jnp.bfloat16)
    low = (np.asarray(table, np.float64) - high.astype(np.float64)).astype(jnp.bfloat16)
    return high, low


def rotation(angle, sign):
    cosine, sine = np.cos(angle), np.sin(angle)
    return np.stack([np.stack([cosine, -sign * sine]), np.stack([sign * sine, cosine])])


def tables():
    angle = 2 * np.pi * (np.arange(NY)[:, None] * KY % NY) / NY
    y_part = np.stack([np.cos(angle), -np.sin(angle)], axis=1)
    y_forward = np.tile(y_part.reshape(NY, 32), (1, 4))
    weight = np.where(KY == 0, 1.0, 2.0) / CELLS
    y_back = np.einsum("ypk,k->pky", y_part, weight).reshape(32, NY)
    z = 4 * np.arange(16)[None, :] + np.arange(4)[:, None]
    angle = 2 * np.pi * (z[:, :, None] * KZ % NZ) / NZ
    z_forward = np.einsum("qpzaj,hH->pzhaqHj", rotation(angle, -1.0), np.eye(2)).reshape(256, 128)
    angle = 2 * np.pi * (z[:, :, None] * KZ % NZ) / NZ
    z_back = np.einsum("qpzaj->qzapj", rotation(angle, 1.0)).reshape(128, 64)
    return y_forward, y_back, z_forward, z_back


Y_FORWARD, Y_BACK, Z_FORWARD, Z_BACK = tables()
PHASE = np.stack([np.cos(2 * np.pi * np.arange(512) / 512), np.sin(2 * np.pi * np.arange(512) / 512)]).astype(np.float32)


def split(values):
    high = values.astype(B16)
    return high, (values - high.astype(F32)).astype(B16)


def dot(left, right):
    return jnp.dot(left, right, preferred_element_type=F32)


def dot_nt(left, right, precision=None):
    return lax.dot_general(left, right, (((1,), (1,)), ((), ())), precision=precision, preferred_element_type=F32)


def dot_exact(left, right):
    return jnp.dot(left, right, precision=EXACT, preferred_element_type=F32)


def iota(shape, axis):
    return lax.broadcasted_iota(jnp.int32, shape, axis)


def phase_index(frequency, block):
    return (frequency * (32 * block + 15)) & 511


def place(frequency):
    return (frequency % 32) // 2, frequency % 2


def cosine(frequency, step):
    return float(np.cos(2 * np.pi * frequency * (step + 0.5) / NX))


def sine(frequency, step):
    return float(np.sin(2 * np.pi * frequency * (step + 0.5) / NX))


def signs(rows, first):
    return jnp.where(iota((rows, 128), 1) < 64, first, -first).astype(F32)


def forward_kernel(
    phase_hbm, field_hbm, weight_hbm, y_hbm, out_ref, sent_ref, kept_ref,
    phase_ref, half_ref, rows_ref, field_ref, weight_ref, small_ref, y_ref, sems,
):
    pa, pb = lax.axis_index("pa"), lax.axis_index("pb")
    copies = [
        pltpu.make_async_copy(source, target, sems.at[number])
        for number, (source, target) in enumerate(
            [
                (y_hbm, small_ref),
                (field_hbm.at[:, 0:128], field_ref.at[0]),
                (field_hbm.at[:, 128:256], field_ref.at[1]),
                (weight_hbm, weight_ref),
                (phase_hbm, phase_ref),
            ]
        )
    ]
    for copy in copies:
        copy.start()
    copies[0].wait()
    small = small_ref[...].reshape(16, 16, 256)
    for xj in range(4):
        mine = (iota((16, 256), 1) % 128 // 32 == xj).astype(F32).astype(B16)
        y_ref[xj] = (small * mine[None]).reshape(256, 256)
    for copy in copies[1:3]:
        copy.wait()
    total = jnp.zeros((256, 128), F32)
    for xj in range(4):
        piece = jnp.concatenate(
            [field_ref[half, pl.ds(xj, 256, stride=4), :] for half in range(2)], axis=1
        )
        high, low = split(piece)
        product = dot(high, y_ref[xj])
        total = total + product[:, 0:128] + product[:, 128:256] + dot(low, y_ref[xj, :, 0:128])
    half_ref[...] = total
    copies[4].wait()
    lines = []
    for x4 in range(4):
        piece = jnp.concatenate([half_ref[pl.ds(z * 4 + x4, 16, stride=16), :] for z in range(4)], axis=0).T
        for xj in range(4):
            lines.append(jnp.concatenate([piece[32 * xj : 32 * xj + 16], piece[32 * xj + 16 : 32 * xj + 32]], axis=1))
    sign = signs(8, 1.0)
    for half in range(2):
        rows = slice(8 * half, 8 * half + 8)
        even = [lines[8 + j][rows] + lines[7 - j][rows] for j in range(8)]
        odd = [pltpu.roll(lines[8 + j][rows] - lines[7 - j][rows], 64, axis=1) * sign for j in range(8)]
        for frequency in range(17):
            first = sum(even[j] * cosine(frequency, j) for j in range(8))
            second = sum(odd[j] * sine(frequency, j) for j in range(8))
            values = {}
            if frequency < 16:
                values[frequency] = first + second
            if frequency > 0:
                values[-frequency] = first - second
            for signed, value in values.items():
                index = phase_index(signed, pb)
                kxp, kxl = place(signed)
                out_ref[pl.ds(kxp * 32 + kxl + 16 * half, 8, stride=2), :] = value * phase_ref[0, index] + pltpu.roll(
                    value, 64, axis=1
                ) * (sign * phase_ref[1, index])
    copies[3].wait()
    rows_ref[:, 0:32] = weight_ref[...]
    for target, wanted in ((sent_ref, jnp.where(pa < 8, 1, 0)), (kept_ref, 0)):
        chosen = rows_ref[pl.ds(wanted, 512, stride=2), :]
        target[...] = jnp.concatenate([chosen[128 * q : 128 * (q + 1), 0:32] for q in range(4)], axis=1)


def local_kernel(
    field_hbm, map_hbm, base_hbm, coef_hbm, index_hbm, y_hbm, gain_hbm, bias_hbm,
    hidden_ref, stat_ref, kan_ref, shift_ref, index_ref, y_ref, gain_ref, bias_ref,
    map_ref, base_ref, coef_ref, field_ref, row_ref, sems,
):
    copies = [
        pltpu.make_async_copy(
            field_hbm.at[:, :, 128 * half : 128 * half + 128],
            field_ref.at[half].reshape(16, PITCH, 128).at[:, 0:64, :],
            sems.at[half],
        )
        for half in range(2)
    ]
    small = [
        pltpu.make_async_copy(source, target, sems.at[2 + number])
        for number, (source, target) in enumerate([(map_hbm, map_ref), (base_hbm, base_ref), (coef_hbm, coef_ref)])
    ] + [
        pltpu.make_async_copy(gain_hbm, row_ref.at[0:1, :], sems.at[8]),
        pltpu.make_async_copy(bias_hbm, row_ref.at[1:2, :], sems.at[9]),
    ]
    moved = [pltpu.make_async_copy(y_hbm, y_ref, sems.at[7])] + [
        pltpu.make_async_copy(
            index_hbm.at[:, :, 128 * half : 128 * half + 128],
            index_ref.at[half].reshape(16, PITCH, 128).at[:, 0:64, :],
            sems.at[5 + half],
        )
        for half in range(2)
    ]
    for copy in small + copies + moved:
        copy.start()
    for copy in small:
        copy.wait()
    last = coef_ref[:, 7, :]
    pieces = [coef_ref[:, basis, :] - last for basis in range(7)] + [base_ref[...]]
    high, low = split(jnp.concatenate(pieces, axis=1))
    kan_ref[0:16, 0:128] = high
    kan_ref[0:16, 128:256] = high
    kan_ref[16:32, 0:128] = low
    kan_ref[16:32, 128:256] = jnp.zeros((16, 128), B16)
    shift_ref[...] = jnp.broadcast_to(jnp.sum(last, axis=1, keepdims=True), (16, 128))
    gain_ref[...] = jnp.broadcast_to(column(row_ref[0:1, :]), (16, 128))
    bias_ref[...] = jnp.broadcast_to(column(row_ref[1:2, :]), (16, 128))
    high, low = split(map_ref[...])
    zero = jnp.zeros((16, 16), B16)
    maps = jnp.concatenate(
        [jnp.concatenate([high, high], axis=1), jnp.concatenate([low, zero], axis=1)], axis=0
    )
    for copy in copies:
        copy.wait()

    def step(x, total):
        for z in range(4):
            rows = pl.ds(z * 16 + x, 16, stride=PITCH)
            high, low = split(jnp.concatenate([field_ref[half, rows, :] for half in range(2)], axis=1))
            both = dot(maps, jnp.concatenate([high, low], axis=0))
            value = both[0:16] + both[16:32]
            total = total + value
            start = pl.multiple_of(x * 64 + z * 16, 16)
            hidden_ref[pl.ds(start, 16), :] = value
        return total

    total = lax.fori_loop(0, 16, step, jnp.zeros((16, 256), F32), unroll=4)
    mean = jnp.sum(total, axis=1, keepdims=True) * (1.0 / BLOCK_CELLS)

    def spread(part, total):
        for z in range(4):
            start = pl.multiple_of(part * 64 + z * 16, 16)
            away = hidden_ref[pl.ds(start, 16), :] - mean
            total = total + away * away
        return total

    total = lax.fori_loop(0, 16, spread, jnp.zeros((16, 256), F32), unroll=4)
    squares = jnp.sum(total, axis=1, keepdims=True)
    first = iota((16, 128), 1) == 0
    stat_ref[0:16, :] = jnp.where(first, mean, 0.0)
    stat_ref[16:32, :] = jnp.where(first, squares, 0.0)
    for copy in moved:
        copy.wait()


def mix_kernel(
    got_ref, partner_ref, kept_ref, stat_ref, phase_hbm, weight_hbm, map_hbm, z_hbm, back_hbm, out_ref,
    phase_ref, map_ref, z_ref, back_ref, rows_ref, weight_ref, both_ref, sems,
):
    pa, pb = lax.axis_index("pa"), lax.axis_index("pb")
    copies = [
        pltpu.make_async_copy(source, target, sems.at[number])
        for number, (source, target) in enumerate(
            [
                (z_hbm, z_ref),
                (map_hbm, map_ref),
                (weight_hbm, weight_ref),
                (back_hbm, back_ref),
                (phase_hbm, phase_ref),
            ]
        )
    ]
    for copy in copies:
        copy.start()
    total = jnp.sum(got_ref[...].reshape(16, 4, 8, 128), axis=1)
    total = total + pltpu.roll(total, 4, axis=1)
    total = total + pltpu.roll(total, 2, axis=1)
    rows_ref[...] = total.reshape(128, 128)
    lines = jnp.concatenate([rows_ref[pl.ds(0, 16, stride=8), :], rows_ref[pl.ds(1, 16, stride=8), :]], axis=0)
    lines = lines.T
    lines = jnp.concatenate([lines[16 * q : 16 * (q + 1)] for q in range(8)], axis=1)
    for copy in copies:
        copy.wait()
    modes = dot_exact(lines, z_ref[...])
    real = [modes[:, 32 * k : 32 * k + 32] for k in range(2)]
    imag = [modes[:, 64 + 32 * k : 96 + 32 * k] for k in range(2)]
    lower = pa < 8
    far_real = jnp.where(lower, real[0], real[1])
    far_imag = jnp.where(lower, imag[0], imag[1])
    odd = iota((32, 32), 0) % 2 == 1
    twice = (iota((32, 16), 0) // 2 == iota((32, 16), 1)).astype(F32)
    map_rows = dot_exact(twice, map_ref[...])
    mixed_real = jnp.zeros((32, 32), F32)
    mixed_imag = jnp.zeros((32, 32), F32)
    local_real = jnp.zeros((32, 32), F32)
    local_imag = jnp.zeros((32, 32), F32)
    partner_real = jnp.zeros((32, 32), F32)
    partner_imag = jnp.zeros((32, 32), F32)
    source, target = iota((128, 128), 0), iota((128, 128), 1)
    turn = jnp.logical_and(source // 32 == target // 32, source % 32 == (32 - target % 32) % 32)
    turn = jnp.logical_and(turn, target % 32 != 16).astype(F32)
    turned = dot_exact(jnp.where(pa == 0, kept_ref[...], partner_ref[...]), turn)
    both_ref[pl.ds(0, 128, stride=2), :] = turned
    both_ref[pl.ds(1, 128, stride=2), :] = turned
    for i in range(16):
        mode_real = jnp.where(odd, real[1][i : i + 1], real[0][i : i + 1])
        mode_imag = jnp.where(odd, imag[1][i : i + 1], imag[0][i : i + 1])
        weight_real = weight_ref[32 * i : 32 * i + 32, :]
        weight_imag = weight_ref[512 + 32 * i : 544 + 32 * i, :]
        mixed_real = mixed_real + weight_real * mode_real - weight_imag * mode_imag
        mixed_imag = mixed_imag + weight_real * mode_imag + weight_imag * mode_real
        column = map_rows[:, i : i + 1]
        local_real = local_real + column * mode_real
        local_imag = local_imag + column * mode_imag
        row = 32 * (i % 8)
        lane = 32 * (i // 8)
        weight_real = both_ref[row : row + 32, lane : lane + 32]
        weight_imag = both_ref[row : row + 32, 64 + lane : 96 + lane]
        mode_real = far_real[i : i + 1]
        mode_imag = far_imag[i : i + 1]
        partner_real = partner_real + weight_real * mode_real + weight_imag * mode_imag
        partner_imag = partner_imag + weight_imag * mode_real - weight_real * mode_imag
    origin = jnp.logical_and(
        jnp.logical_and(pa == 0, pb == 0), jnp.logical_and(iota((32, 32), 0) % 2 == 0, iota((32, 32), 1) == 0)
    )
    centre = jnp.where(origin, mixed_real, 0.0)
    moved_real = jnp.where(origin, 0.0, mixed_real)
    moved_imag = jnp.where(origin, 0.0, mixed_imag)
    own = jnp.where(pb == 0, 0.5, 2.0)
    cross = jnp.where(pb == 0, 2.0, 4.0)
    power = own * (moved_real * moved_real + moved_imag * moved_imag)
    power = power + cross * (moved_real * local_real + moved_imag * local_imag)
    pair = moved_real * partner_real - moved_imag * partner_imag
    chosen = jnp.where(lower, 0, 1)
    pair = jnp.where(
        jnp.logical_and(pb == 0, iota((32, 32), 0) % 2 == chosen), jnp.where(pa == 0, 0.5, 1.0) * pair, 0.0
    )
    power = power + pair
    sums = jnp.concatenate(
        [
            power * (1.0 / CELLS),
            jnp.zeros((16, 32), F32),
            stat_ref[:, 0:32],
            centre * (1.0 / CELLS),
            jnp.zeros((16, 32), F32),
        ],
        axis=0,
    )
    sums = dot_nt(jnp.ones((8, 32), F32), sums, EXACT)
    out_ref[pl.ds(2, 256, stride=3), :] = jnp.broadcast_to(sums[0:1], (256, 128))
    order = (iota((32, 32), 1) == 2 * (iota((32, 32), 0) % 16) + iota((32, 32), 0) // 16).astype(F32)
    mixed = dot_exact(order, jnp.concatenate([mixed_real, mixed_imag], axis=1))
    planes = dot_nt(back_ref[...], mixed, EXACT)
    sign = signs(16, -1.0)
    for kxl in range(2):
        frequency = 2 * pa + kxl - jnp.where(lower, 0, 32)
        value = jnp.concatenate(
            [planes[16 * q : 16 * (q + 1), 16 * kxl : 16 * kxl + 16] for q in range(8)], axis=1
        )
        other = pltpu.roll(value, 64, axis=1) * sign
        for block in range(16):
            index = phase_index(frequency, block)
            out_ref[pl.ds(block * 3 + kxl, 16, stride=48), :] = (
                value * phase_ref[0, index] + other * phase_ref[1, index]
            )


def column(row):
    eye = (iota((16, 16), 0) == iota((16, 16), 1)).astype(F32)
    return dot_nt(eye, jnp.broadcast_to(row, (8, 16)), EXACT)[:, 0:1]


def output_kernel(
    got_ref, hidden_ref, kan_ref, constant_ref, index_ref, small_ref, gain_ref, bias_ref, out_ref,
    y_high_ref, y_low_ref, spec_ref, result_ref, sems,
):
    stats = got_ref[pl.ds(2, 256, stride=3), :]
    sums = jnp.sum(stats, axis=0, keepdims=True)
    mean = sums * (1.0 / 256)
    away = stats - mean
    between = jnp.sum(away * away, axis=0, keepdims=True) * float(BLOCK_CELLS)
    lane = iota((1, 128), 1)
    is_mean = jnp.logical_and(lane >= 48, lane < 64)
    is_centre = jnp.logical_and(lane >= 80, lane < 112)
    variance = jnp.where(is_mean, between, jnp.where(lane < 80, sums, 0.0)) * (1.0 / CELLS)
    mean = jnp.where(is_mean, mean, jnp.where(is_centre, sums, 0.0))
    lane, row = iota((16, 128), 1), iota((16, 128), 0)
    owner = jnp.where(
        lane < 32, lane // 2, jnp.where(lane < 80, lane % 16, jnp.where(lane < 112, (lane - 80) // 2, -1))
    )
    pick = (owner == row).astype(F32)
    mean = dot_nt(pick, jnp.broadcast_to(mean, (8, 128)), EXACT)[:, 0:1]
    variance = dot_nt(pick, jnp.broadcast_to(variance, (8, 128)), EXACT)[:, 0:1]
    scale = gain_ref[:, 0:1] * lax.rsqrt(variance + EPSILON)
    mean = jnp.broadcast_to(jnp.concatenate([mean] * 4, axis=0), (64, 128))
    scale = jnp.broadcast_to(jnp.concatenate([scale] * 4, axis=0), (64, 128))
    bias = jnp.broadcast_to(jnp.concatenate([bias_ref[:, 0:1]] * 4, axis=0), (64, 128))
    lines = [[None] * 2 for _ in range(16)]
    sign = signs(8, -1.0)
    for half in range(2):
        modes = {}
        for frequency in range(-16, 16):
            kxp, kxl = place(frequency)
            modes[frequency] = got_ref[pl.ds(kxp * 48 + kxl + 24 * half, 8, stride=3), :]
        even = [modes[k] + modes[-k] for k in range(1, 16)] + [modes[-16]]
        odd = [modes[k] - modes[-k] for k in range(1, 16)] + [-modes[-16]]
        odd = [pltpu.roll(value, 64, axis=1) * sign for value in odd]
        for j in range(8):
            first = modes[0] + sum(even[k - 1] * cosine(k, j) for k in range(1, 17))
            second = sum(odd[k - 1] * sine(k, j) for k in range(1, 17))
            lines[8 + j][half] = first + second
            lines[7 - j][half] = first - second
    groups = []
    for x4 in range(4):
        piece = jnp.concatenate([lines[4 * x4 + xj][half] for xj in range(4) for half in range(2)], axis=0).T
        groups.append(jnp.concatenate([piece[0:64], piece[64:128]], axis=1))
    high, low = split(jnp.concatenate(groups, axis=0))
    both = jnp.concatenate([high, low], axis=0)
    for number, table in enumerate((y_high_ref, y_low_ref)):
        table[...] = jnp.zeros((4, 128, 256), B16)
        for xj in range(4):
            for part in range(2):
                start = 32 * number + 16 * part
                row = 64 * part + 16 * xj
                table[xj, row : row + 16, :] = small_ref[start : start + 16, :]
    for xj in range(4):
        product = dot(both, y_high_ref[xj])
        value = product[0:256] + product[256:512] + dot(high, y_low_ref[xj])
        for x4 in range(4):
            start = (4 * x4 + xj) * 64
            spec_ref[start : start + 64, :] = value[64 * x4 : 64 * x4 + 64]
    weights = kan_ref[...]
    constant = constant_ref[...]
    copies = []
    for half in range(2):
        lanes = slice(128 * half, 128 * half + 128)

        def step(x, carry, half=half, lanes=lanes):
            rows = pl.ds(pl.multiple_of(x * 64, 64), 64)
            hidden = spec_ref[rows, lanes] + hidden_ref[rows, lanes]
            normed = (hidden - mean) * scale + bias
            level = jnp.concatenate(
                [index_ref[half, pl.ds(z * 16 + x, 16, stride=PITCH), :] for z in range(4)], axis=0
            ).astype(F32)
            local = jnp.clip(normed * 1.25 + (2.5 - level), 0.0, 1.0)
            other = 1.0 - local
            square = local * local
            cube = square * local
            p0 = other * other * other * (1.0 / 6.0)
            p3 = cube * (1.0 / 6.0)
            p1 = 0.5 * cube - square + 2.0 / 3.0
            p2 = 0.5 * (square + local - cube) + 1.0 / 6.0
            level = level.astype(B16)
            at = [level == jnp.asarray(k, B16) for k in range(5)]
            zero = jnp.zeros((64, 128), B16)
            pieces = [split(piece) for piece in (p0, p1, p2, p3)]
            parts = []
            for basis in range(7):
                value = [zero, zero]
                for r in range(4):
                    if 0 <= basis - r <= 4:
                        value = [jnp.where(at[basis - r], pieces[r][k], value[k]) for k in range(2)]
                parts.append(value)
            parts.append(split(0.5 * normed * (1.0 + jnp.tanh(0.5 * normed))))
            columns = []
            for z in range(4):
                columns.append(
                    jnp.concatenate(
                        [part[0][16 * z : 16 * z + 16] for part in parts]
                        + [part[1][16 * z : 16 * z + 16] for part in parts],
                        axis=0,
                    )
                )
            product = dot(weights, jnp.concatenate(columns, axis=1))
            for z in range(4):
                value = product[0:16, 128 * z : 128 * z + 128] + product[16:32, 128 * z : 128 * z + 128]
                result_ref[half, pl.ds(z * 16 + x, 16, stride=PITCH), :] = value + constant
            return carry

        for part in range(2):
            lax.fori_loop(8 * part, 8 * part + 8, step, 0, unroll=8)
            for z in range(4):
                row = 16 * z + 8 * part
                copy = pltpu.make_async_copy(
                    result_ref.at[half].reshape(16, PITCH, 128).at[:, row : row + 8, :],
                    out_ref.at[:, row : row + 8, lanes],
                    sems.at[8 * half + 4 * part + z],
                )
                copy.start()
                copies.append(copy)
    for copy in copies:
        copy.wait()


def whole():
    return pl.BlockSpec(memory_space=pltpu.VMEM)


def scalars():
    return pl.BlockSpec(memory_space=pltpu.SMEM)


def hbm():
    return pl.BlockSpec(memory_space=pltpu.HBM)


def params(vmem):
    return pltpu.CompilerParams(vmem_limit_bytes=vmem * MIB)


def cost(flops, moved):
    return pl.CostEstimate(flops=flops, bytes_accessed=moved, transcendentals=0)


def shape(dims, dtype=F32):
    return jax.ShapeDtypeStruct(dims, dtype)


def far(*arrays):
    return [pltpu.with_memory_space_constraint(array, pltpu.HBM) for array in arrays]


def near(*arrays):
    return [pltpu.with_memory_space_constraint(array, pltpu.VMEM) for array in arrays]


def transfers(count):
    return pltpu.SemaphoreType.DMA((count,))


def forward_call(field, weight):
    y_high, y_low = split_table(Y_FORWARD)
    return pl.pallas_call(
        forward_kernel,
        out_shape=(pltpu.VMEM((512, 128), F32), pltpu.VMEM((128, 128), F32), pltpu.VMEM((128, 128), F32)),
        in_specs=[hbm()] * 4,
        out_specs=(whole(),) * 3,
        scratch_shapes=[
            pltpu.SMEM((2, 512), F32),
            pltpu.VMEM((256, 128), F32),
            pltpu.VMEM((1024, 128), F32),
            pltpu.VMEM((2, 1024, 128), F32),
            pltpu.VMEM((1024, 32), F32),
            pltpu.VMEM((256, 256), B16),
            pltpu.VMEM((4, 256, 256), B16),
            transfers(5),
        ],
        compiler_params=params(24),
        cost_estimate=cost(4 * 10**8, 4 * 10**6),
        name="forward",
    )(
        *far(jnp.asarray(PHASE), field, weight, jnp.asarray(np.concatenate([y_high, y_low], axis=1)))
    )


def local_call(field, local_weight, base_weight, spline_coef, index, bn_gain, bn_shift):
    y_table = np.concatenate(split_table(Y_BACK), axis=0)
    return pl.pallas_call(
        local_kernel,
        out_shape=(
            pltpu.VMEM((1024, 256), F32), pltpu.VMEM((32, 128), F32), pltpu.VMEM((32, 256), B16), pltpu.VMEM((16, 128), F32),
            pltpu.VMEM((2, 16 * PITCH, 128), jnp.int32),
            pltpu.VMEM((64, 256), B16),
            pltpu.VMEM((16, 128), F32),
            pltpu.VMEM((16, 128), F32),
        ),
        in_specs=[hbm()] * 8,
        out_specs=(whole(),) * 8,
        scratch_shapes=[
            pltpu.VMEM((16, 16), F32),
            pltpu.VMEM((16, 16), F32),
            pltpu.VMEM((16, 8, 16), F32),
            pltpu.VMEM((2, 16 * PITCH, 128), F32),
            pltpu.VMEM((2, 16), F32),
            transfers(10),
        ],
        compiler_params=params(24),
        cost_estimate=cost(10**8, 2 * 10**6),
        name="local",
    )(*far(field.reshape(16, 64, 256), local_weight, base_weight, jnp.transpose(spline_coef, (0, 2, 1)), index.reshape(16, 64, 256),
            jnp.asarray(y_table), bn_gain.reshape(1, 16), bn_shift.reshape(1, 16)))


def mix_call(got, weight, partner, kept, local_weight, stat):
    return pl.pallas_call(
        mix_kernel,
        out_shape=pltpu.VMEM((768, 128), F32),
        in_specs=[whole()] * 4 + [hbm()] * 5,
        out_specs=whole(),
        scratch_shapes=[
            pltpu.SMEM((2, 512), F32),
            pltpu.VMEM((16, 16), F32),
            pltpu.VMEM((256, 128), F32),
            pltpu.VMEM((128, 64), F32),
            pltpu.VMEM((128, 128), F32),
            pltpu.VMEM((1024, 32), F32),
            pltpu.VMEM((256, 128), F32),
            transfers(5),
        ],
        compiler_params=params(24),
        cost_estimate=cost(10**7, 10**6),
        name="mix",
    )(
        *near(got, partner, kept, stat),
        *far(jnp.asarray(PHASE), weight, local_weight, jnp.asarray(Z_FORWARD, F32), jnp.asarray(Z_BACK, F32)),
    )


def output_call(back, hidden, kan, constant, index, y_table, gain, bias):
    return pl.pallas_call(
        output_kernel,
        out_shape=pltpu.HBM((16, 64, 256), F32),
        in_specs=[whole()] * 8,
        out_specs=hbm(),
        scratch_shapes=[
            pltpu.VMEM((4, 128, 256), B16),
            pltpu.VMEM((4, 128, 256), B16),
            pltpu.VMEM((1024, 256), F32),
            pltpu.VMEM((2, 16 * PITCH, 128), F32),
            transfers(16),
        ],
        compiler_params=params(24),
        cost_estimate=cost(10**9, 6 * 10**6),
        name="output",
    )(*near(back, hidden, kan, constant, index, y_table, gain, bias))


def on_device(
    field, spline_index, spec_weight, local_weight, bn_gain, bn_shift, base_weight, spline_coef
):
    field = field.reshape(1024, 256)
    index = spline_index.reshape(1024, 256)
    weight = jnp.transpose(spec_weight, (0, 1, 2, 4, 5, 3)).reshape(1024, 32)
    sent, own, kept = forward_call(field, weight)
    path = [0]
    while path[-1] != 8:
        path.append(15 - path[-1] if path[-1] < 8 else 16 - path[-1])
    partner = lax.ppermute(own, BOTH, [(16 * a, 16 * b) for a, b in zip(path[:-1], path[1:])])
    got = lax.all_to_all(sent.reshape(256, 2, 128), BOTH, 0, 0, tiled=True).reshape(512, 128)
    hidden, stat, *rest = local_call(
        field, local_weight, base_weight, spline_coef, index, bn_gain, bn_shift
    )
    back = mix_call(got, weight, partner, kept, local_weight, stat)
    back = lax.all_to_all(back.reshape(256, 1, 384), BOTH, 0, 0, tiled=True).reshape(768, 128)
    output = output_call(back, hidden, *rest)
    return output.reshape(16, 4, 16, 256)


def solution(mesh):
    in_specs = (
        P(None, "pa", "pb", None),
        P(None, "pa", "pb", None),
        P(None, None, None, None, "pa", "pb"),
        P(),
        P(),
        P(),
        P(),
        P(),
    )
    out_specs = P(None, "pa", "pb", None)
    return jax.shard_map(
        on_device, mesh=mesh, in_specs=in_specs, out_specs=out_specs, check_vma=False
    )
```

```python
import jax
import jax.numpy as jnp
import numpy as np
from jax import lax
from jax.experimental import pallas as pl
from jax.experimental.pallas import tpu as pltpu
from jax.sharding import PartitionSpec as P

NZ, NX, NY = 64, 256, 256
CELLS = NZ * NX * NY
BLOCK_CELLS = 4 * 16 * 256
EPSILON = 1e-05
EXACT = lax.Precision.HIGHEST
F32 = jnp.float32
B16 = jnp.bfloat16
BOTH = ("pa", "pb")
MIB = 1024 * 1024
PITCH = 72

KZ = np.array([j if j < 16 else j - 32 for j in range(32)])
KY = np.arange(16)


def split_table(table):
    high = jnp.asarray(table, F32).astype(B16)
    high = np.asarray(table, np.float32).astype(jnp.bfloat16)
    low = (np.asarray(table, np.float64) - high.astype(np.float64)).astype(jnp.bfloat16)
    return high, low


def rotation(angle, sign):
    cosine, sine = np.cos(angle), np.sin(angle)
    return np.stack([np.stack([cosine, -sign * sine]), np.stack([sign * sine, cosine])])


def tables():
    angle = 2 * np.pi * (np.arange(NY)[:, None] * KY % NY) / NY
    y_part = np.stack([np.cos(angle), -np.sin(angle)], axis=1)
    y_forward = np.tile(y_part.reshape(NY, 32), (1, 4))
    weight = np.where(KY == 0, 1.0, 2.0) / CELLS
    y_back = np.einsum("ypk,k->pky", y_part, weight).reshape(32, NY)
    z = 4 * np.arange(16)[None, :] + np.arange(4)[:, None]
    angle = 2 * np.pi * (z[:, :, None] * KZ % NZ) / NZ
    z_forward = np.einsum("qpzaj,hH->pzhaqHj", rotation(angle, -1.0), np.eye(2)).reshape(256, 128)
    angle = 2 * np.pi * (z[:, :, None] * KZ % NZ) / NZ
    z_back = np.einsum("qpzaj->qzapj", rotation(angle, 1.0)).reshape(128, 64)
    return y_forward, y_back, z_forward, z_back


Y_FORWARD, Y_BACK, Z_FORWARD, Z_BACK = tables()
PHASE = np.stack([np.cos(2 * np.pi * np.arange(512) / 512), np.sin(2 * np.pi * np.arange(512) / 512)]).astype(np.float32)


def split(values):
    high = values.astype(B16)
    return high, (values - high.astype(F32)).astype(B16)


def dot(left, right):
    return jnp.dot(left, right, preferred_element_type=F32)


def dot_nt(left, right, precision=None):
    return lax.dot_general(left, right, (((1,), (1,)), ((), ())), precision=precision, preferred_element_type=F32)


def dot_exact(left, right):
    return jnp.dot(left, right, precision=EXACT, preferred_element_type=F32)


def iota(shape, axis):
    return lax.broadcasted_iota(jnp.int32, shape, axis)


def phase_index(frequency, block):
    return (frequency * (32 * block + 15)) & 511


def place(frequency):
    return (frequency % 32) // 2, frequency % 2


def cosine(frequency, step):
    return float(np.cos(2 * np.pi * frequency * (step + 0.5) / NX))


def sine(frequency, step):
    return float(np.sin(2 * np.pi * frequency * (step + 0.5) / NX))


def signs(rows, first):
    return jnp.where(iota((rows, 128), 1) < 64, first, -first).astype(F32)


def forward_kernel(
    phase_hbm, field_hbm, weight_hbm, y_hbm, out_ref, sent_ref, kept_ref,
    phase_ref, half_ref, rows_ref, field_ref, weight_ref, small_ref, y_ref, sems,
):
    pa, pb = lax.axis_index("pa"), lax.axis_index("pb")
    copies = [
        pltpu.make_async_copy(source, target, sems.at[number])
        for number, (source, target) in enumerate(
            [
                (y_hbm, small_ref),
                (field_hbm.at[:, 0:128], field_ref.at[0]),
                (field_hbm.at[:, 128:256], field_ref.at[1]),
                (weight_hbm, weight_ref),
                (phase_hbm, phase_ref),
            ]
        )
    ]
    for copy in copies:
        copy.start()
    copies[0].wait()
    small = small_ref[...].reshape(16, 16, 256)
    for xj in range(4):
        mine = (iota((16, 256), 1) % 128 // 32 == xj).astype(F32).astype(B16)
        y_ref[xj] = (small * mine[None]).reshape(256, 256)
    for copy in copies[1:3]:
        copy.wait()
    total = jnp.zeros((256, 128), F32)
    for xj in range(4):
        piece = jnp.concatenate(
            [field_ref[half, pl.ds(xj, 256, stride=4), :] for half in range(2)], axis=1
        )
        high, low = split(piece)
        product = dot(high, y_ref[xj])
        total = total + product[:, 0:128] + product[:, 128:256] + dot(low, y_ref[xj, :, 0:128])
    half_ref[...] = total
    copies[4].wait()
    lines = []
    for x4 in range(4):
        piece = jnp.concatenate([half_ref[pl.ds(z * 4 + x4, 16, stride=16), :] for z in range(4)], axis=0).T
        for xj in range(4):
            lines.append(jnp.concatenate([piece[32 * xj : 32 * xj + 16], piece[32 * xj + 16 : 32 * xj + 32]], axis=1))
    sign = signs(8, 1.0)
    for half in range(2):
        rows = slice(8 * half, 8 * half + 8)
        even = [lines[8 + j][rows] + lines[7 - j][rows] for j in range(8)]
        odd = [pltpu.roll(lines[8 + j][rows] - lines[7 - j][rows], 64, axis=1) * sign for j in range(8)]
        for frequency in range(17):
            first = sum(even[j] * cosine(frequency, j) for j in range(8))
            second = sum(odd[j] * sine(frequency, j) for j in range(8))
            values = {}
            if frequency < 16:
                values[frequency] = first + second
            if frequency > 0:
                values[-frequency] = first - second
            for signed, value in values.items():
                index = phase_index(signed, pb)
                kxp, kxl = place(signed)
                out_ref[pl.ds(kxp * 32 + kxl + 16 * half, 8, stride=2), :] = value * phase_ref[0, index] + pltpu.roll(
                    value, 64, axis=1
                ) * (sign * phase_ref[1, index])
    copies[3].wait()
    rows_ref[:, 0:32] = weight_ref[...]
    for target, wanted in ((sent_ref, jnp.where(pa < 8, 1, 0)), (kept_ref, 0)):
        chosen = rows_ref[pl.ds(wanted, 512, stride=2), :]
        target[...] = jnp.concatenate([chosen[128 * q : 128 * (q + 1), 0:32] for q in range(4)], axis=1)


def local_kernel(
    field_hbm, map_hbm, base_hbm, coef_hbm, index_hbm, y_hbm, gain_hbm, bias_hbm, z_hbm, back_hbm,
    z_ref, back_ref, map_ref, hidden_ref, stat_ref, kan_ref, shift_ref, index_ref, y_ref, gain_ref, bias_ref,
    base_ref, coef_ref, field_ref, row_ref, sems,
):
    copies = [
        pltpu.make_async_copy(
            field_hbm.at[:, :, 128 * half : 128 * half + 128],
            field_ref.at[half].reshape(16, PITCH, 128).at[:, 0:64, :],
            sems.at[half],
        )
        for half in range(2)
    ]
    small = [
        pltpu.make_async_copy(source, target, sems.at[2 + number])
        for number, (source, target) in enumerate([(map_hbm, map_ref), (base_hbm, base_ref), (coef_hbm, coef_ref)])
    ] + [
        pltpu.make_async_copy(gain_hbm, row_ref.at[0:1, :], sems.at[8]),
        pltpu.make_async_copy(bias_hbm, row_ref.at[1:2, :], sems.at[9]),
    ]
    moved = [
        pltpu.make_async_copy(y_hbm, y_ref, sems.at[7]),
        pltpu.make_async_copy(z_hbm, z_ref, sems.at[10]),
        pltpu.make_async_copy(back_hbm, back_ref, sems.at[11]),
    ] + [
        pltpu.make_async_copy(
            index_hbm.at[:, :, 128 * half : 128 * half + 128],
            index_ref.at[half].reshape(16, PITCH, 128).at[:, 0:64, :],
            sems.at[5 + half],
        )
        for half in range(2)
    ]
    for copy in small + copies + moved:
        copy.start()
    for copy in small:
        copy.wait()
    last = coef_ref[:, 7, :]
    pieces = [coef_ref[:, basis, :] - last for basis in range(7)] + [base_ref[...]]
    high, low = split(jnp.concatenate(pieces, axis=1))
    kan_ref[0:16, 0:128] = high
    kan_ref[0:16, 128:256] = high
    kan_ref[16:32, 0:128] = low
    kan_ref[16:32, 128:256] = jnp.zeros((16, 128), B16)
    shift_ref[...] = jnp.broadcast_to(jnp.sum(last, axis=1, keepdims=True), (16, 128))
    gain_ref[...] = jnp.broadcast_to(column(row_ref[0:1, :]), (16, 128))
    bias_ref[...] = jnp.broadcast_to(column(row_ref[1:2, :]), (16, 128))
    high, low = split(map_ref[...])
    zero = jnp.zeros((16, 16), B16)
    maps = jnp.concatenate(
        [jnp.concatenate([high, high], axis=1), jnp.concatenate([low, zero], axis=1)], axis=0
    )
    for copy in copies:
        copy.wait()

    def step(x, total):
        for z in range(4):
            rows = pl.ds(z * 16 + x, 16, stride=PITCH)
            high, low = split(jnp.concatenate([field_ref[half, rows, :] for half in range(2)], axis=1))
            both = dot(maps, jnp.concatenate([high, low], axis=0))
            value = both[0:16] + both[16:32]
            total = total + value
            start = pl.multiple_of(x * 64 + z * 16, 16)
            hidden_ref[pl.ds(start, 16), :] = value
        return total

    total = lax.fori_loop(0, 16, step, jnp.zeros((16, 256), F32), unroll=4)
    mean = jnp.sum(total, axis=1, keepdims=True) * (1.0 / BLOCK_CELLS)

    def spread(part, total):
        for z in range(4):
            start = pl.multiple_of(part * 64 + z * 16, 16)
            away = hidden_ref[pl.ds(start, 16), :] - mean
            total = total + away * away
        return total

    total = lax.fori_loop(0, 16, spread, jnp.zeros((16, 256), F32), unroll=4)
    squares = jnp.sum(total, axis=1, keepdims=True)
    first = iota((16, 128), 1) == 0
    stat_ref[0:16, :] = jnp.where(first, mean, 0.0)
    stat_ref[16:32, :] = jnp.where(first, squares, 0.0)
    for copy in moved:
        copy.wait()


def mix_kernel(
    got_ref, partner_ref, kept_ref, z_ref, back_ref, map_ref, stat_ref, phase_hbm, weight_hbm, out_ref,
    phase_ref, rows_ref, weight_ref, both_ref, sems,
):
    pa, pb = lax.axis_index("pa"), lax.axis_index("pb")
    copies = [
        pltpu.make_async_copy(source, target, sems.at[number])
        for number, (source, target) in enumerate(
            [
                (weight_hbm, weight_ref),
                (phase_hbm, phase_ref),
            ]
        )
    ]
    for copy in copies:
        copy.start()
    total = jnp.sum(got_ref[...].reshape(16, 4, 8, 128), axis=1)
    total = total + pltpu.roll(total, 4, axis=1)
    total = total + pltpu.roll(total, 2, axis=1)
    rows_ref[...] = total.reshape(128, 128)
    lines = jnp.concatenate([rows_ref[pl.ds(0, 16, stride=8), :], rows_ref[pl.ds(1, 16, stride=8), :]], axis=0)
    lines = lines.T
    lines = jnp.concatenate([lines[16 * q : 16 * (q + 1)] for q in range(8)], axis=1)
    modes = dot_exact(lines, z_ref[...])
    real = [modes[:, 32 * k : 32 * k + 32] for k in range(2)]
    imag = [modes[:, 64 + 32 * k : 96 + 32 * k] for k in range(2)]
    lower = pa < 8
    far_real = jnp.where(lower, real[0], real[1])
    far_imag = jnp.where(lower, imag[0], imag[1])
    odd = iota((32, 32), 0) % 2 == 1
    twice = (iota((32, 16), 0) // 2 == iota((32, 16), 1)).astype(F32)
    map_rows = dot_exact(twice, map_ref[...])
    mixed_real = jnp.zeros((32, 32), F32)
    mixed_imag = jnp.zeros((32, 32), F32)
    local_real = jnp.zeros((32, 32), F32)
    local_imag = jnp.zeros((32, 32), F32)
    partner_real = jnp.zeros((32, 32), F32)
    partner_imag = jnp.zeros((32, 32), F32)
    copies[0].wait()
    source, target = iota((128, 128), 0), iota((128, 128), 1)
    turn = jnp.logical_and(source // 32 == target // 32, source % 32 == (32 - target % 32) % 32)
    turn = jnp.logical_and(turn, target % 32 != 16).astype(F32)
    turned = dot_exact(jnp.where(pa == 0, kept_ref[...], partner_ref[...]), turn)
    both_ref[pl.ds(0, 128, stride=2), :] = turned
    both_ref[pl.ds(1, 128, stride=2), :] = turned
    for i in range(16):
        mode_real = jnp.where(odd, real[1][i : i + 1], real[0][i : i + 1])
        mode_imag = jnp.where(odd, imag[1][i : i + 1], imag[0][i : i + 1])
        weight_real = weight_ref[32 * i : 32 * i + 32, :]
        weight_imag = weight_ref[512 + 32 * i : 544 + 32 * i, :]
        mixed_real = mixed_real + weight_real * mode_real - weight_imag * mode_imag
        mixed_imag = mixed_imag + weight_real * mode_imag + weight_imag * mode_real
        column = map_rows[:, i : i + 1]
        local_real = local_real + column * mode_real
        local_imag = local_imag + column * mode_imag
        row = 32 * (i % 8)
        lane = 32 * (i // 8)
        weight_real = both_ref[row : row + 32, lane : lane + 32]
        weight_imag = both_ref[row : row + 32, 64 + lane : 96 + lane]
        mode_real = far_real[i : i + 1]
        mode_imag = far_imag[i : i + 1]
        partner_real = partner_real + weight_real * mode_real + weight_imag * mode_imag
        partner_imag = partner_imag + weight_imag * mode_real - weight_real * mode_imag
    origin = jnp.logical_and(
        jnp.logical_and(pa == 0, pb == 0), jnp.logical_and(iota((32, 32), 0) % 2 == 0, iota((32, 32), 1) == 0)
    )
    centre = jnp.where(origin, mixed_real, 0.0)
    moved_real = jnp.where(origin, 0.0, mixed_real)
    moved_imag = jnp.where(origin, 0.0, mixed_imag)
    own = jnp.where(pb == 0, 0.5, 2.0)
    cross = jnp.where(pb == 0, 2.0, 4.0)
    power = own * (moved_real * moved_real + moved_imag * moved_imag)
    power = power + cross * (moved_real * local_real + moved_imag * local_imag)
    pair = moved_real * partner_real - moved_imag * partner_imag
    chosen = jnp.where(lower, 0, 1)
    pair = jnp.where(
        jnp.logical_and(pb == 0, iota((32, 32), 0) % 2 == chosen), jnp.where(pa == 0, 0.5, 1.0) * pair, 0.0
    )
    power = power + pair
    sums = jnp.concatenate(
        [
            power * (1.0 / CELLS),
            jnp.zeros((16, 32), F32),
            stat_ref[:, 0:32],
            centre * (1.0 / CELLS),
            jnp.zeros((16, 32), F32),
        ],
        axis=0,
    )
    sums = dot_nt(jnp.ones((8, 32), F32), sums, EXACT)
    out_ref[pl.ds(2, 256, stride=3), :] = jnp.broadcast_to(sums[0:1], (256, 128))
    order = (iota((32, 32), 1) == 2 * (iota((32, 32), 0) % 16) + iota((32, 32), 0) // 16).astype(F32)
    mixed = dot_exact(order, jnp.concatenate([mixed_real, mixed_imag], axis=1))
    copies[1].wait()
    planes = dot_nt(back_ref[...], mixed, EXACT)
    sign = signs(16, -1.0)
    for kxl in range(2):
        frequency = 2 * pa + kxl - jnp.where(lower, 0, 32)
        value = jnp.concatenate(
            [planes[16 * q : 16 * (q + 1), 16 * kxl : 16 * kxl + 16] for q in range(8)], axis=1
        )
        other = pltpu.roll(value, 64, axis=1) * sign
        for block in range(16):
            index = phase_index(frequency, block)
            out_ref[pl.ds(block * 3 + kxl, 16, stride=48), :] = (
                value * phase_ref[0, index] + other * phase_ref[1, index]
            )


def column(row):
    eye = (iota((16, 16), 0) == iota((16, 16), 1)).astype(F32)
    return dot_nt(eye, jnp.broadcast_to(row, (8, 16)), EXACT)[:, 0:1]


def output_kernel(
    got_ref, hidden_ref, kan_ref, constant_ref, index_ref, small_ref, gain_ref, bias_ref, out_ref,
    y_high_ref, y_low_ref, spec_ref, result_ref, sems,
):
    stats = got_ref[pl.ds(2, 256, stride=3), :]
    sums = jnp.sum(stats, axis=0, keepdims=True)
    mean = sums * (1.0 / 256)
    away = stats - mean
    between = jnp.sum(away * away, axis=0, keepdims=True) * float(BLOCK_CELLS)
    lane = iota((1, 128), 1)
    is_mean = jnp.logical_and(lane >= 48, lane < 64)
    is_centre = jnp.logical_and(lane >= 80, lane < 112)
    variance = jnp.where(is_mean, between, jnp.where(lane < 80, sums, 0.0)) * (1.0 / CELLS)
    mean = jnp.where(is_mean, mean, jnp.where(is_centre, sums, 0.0))
    lane, row = iota((16, 128), 1), iota((16, 128), 0)
    owner = jnp.where(
        lane < 32, lane // 2, jnp.where(lane < 80, lane % 16, jnp.where(lane < 112, (lane - 80) // 2, -1))
    )
    pick = (owner == row).astype(F32)
    mean = dot_nt(pick, jnp.broadcast_to(mean, (8, 128)), EXACT)[:, 0:1]
    variance = dot_nt(pick, jnp.broadcast_to(variance, (8, 128)), EXACT)[:, 0:1]
    scale = gain_ref[:, 0:1] * lax.rsqrt(jnp.maximum(variance, 0.0) + EPSILON)
    mean = jnp.broadcast_to(jnp.concatenate([mean] * 4, axis=0), (64, 128))
    scale = jnp.broadcast_to(jnp.concatenate([scale] * 4, axis=0), (64, 128))
    bias = jnp.broadcast_to(jnp.concatenate([bias_ref[:, 0:1]] * 4, axis=0), (64, 128))
    lines = [[None] * 2 for _ in range(16)]
    sign = signs(8, -1.0)
    for half in range(2):
        modes = {}
        for frequency in range(-16, 16):
            kxp, kxl = place(frequency)
            modes[frequency] = got_ref[pl.ds(kxp * 48 + kxl + 24 * half, 8, stride=3), :]
        even = [modes[k] + modes[-k] for k in range(1, 16)] + [modes[-16]]
        odd = [modes[k] - modes[-k] for k in range(1, 16)] + [-modes[-16]]
        odd = [pltpu.roll(value, 64, axis=1) * sign for value in odd]
        for j in range(8):
            first = modes[0] + sum(even[k - 1] * cosine(k, j) for k in range(1, 17))
            second = sum(odd[k - 1] * sine(k, j) for k in range(1, 17))
            lines[8 + j][half] = first + second
            lines[7 - j][half] = first - second
    groups = []
    for x4 in range(4):
        piece = jnp.concatenate([lines[4 * x4 + xj][half] for xj in range(4) for half in range(2)], axis=0).T
        groups.append(jnp.concatenate([piece[0:64], piece[64:128]], axis=1))
    high, low = split(jnp.concatenate(groups, axis=0))
    both = jnp.concatenate([high, low], axis=0)
    for number, table in enumerate((y_high_ref, y_low_ref)):
        table[...] = jnp.zeros((4, 128, 256), B16)
        for xj in range(4):
            for part in range(2):
                start = 32 * number + 16 * part
                row = 64 * part + 16 * xj
                table[xj, row : row + 16, :] = small_ref[start : start + 16, :]
    for xj in range(4):
        product = dot(both, y_high_ref[xj])
        value = product[0:256] + product[256:512] + dot(high, y_low_ref[xj])
        for x4 in range(4):
            start = (4 * x4 + xj) * 64
            spec_ref[start : start + 64, :] = value[64 * x4 : 64 * x4 + 64]
    weights = kan_ref[...]
    constant = constant_ref[...]
    copies = []
    for half in range(2):
        lanes = slice(128 * half, 128 * half + 128)

        def step(x, carry, half=half, lanes=lanes):
            rows = pl.ds(pl.multiple_of(x * 64, 64), 64)
            hidden = spec_ref[rows, lanes] + hidden_ref[rows, lanes]
            normed = (hidden - mean) * scale + bias
            level = jnp.concatenate(
                [index_ref[half, pl.ds(z * 16 + x, 16, stride=PITCH), :] for z in range(4)], axis=0
            ).astype(F32)
            local = jnp.clip(normed * 1.25 + (2.5 - level), 0.0, 1.0)
            other = 1.0 - local
            square = local * local
            cube = square * local
            p0 = other * other * other * (1.0 / 6.0)
            p3 = cube * (1.0 / 6.0)
            p1 = 0.5 * cube - square + 2.0 / 3.0
            p2 = 0.5 * (square + local - cube) + 1.0 / 6.0
            level = level.astype(B16)
            at = [level == jnp.asarray(k, B16) for k in range(5)]
            zero = jnp.zeros((64, 128), B16)
            pieces = [split(piece) for piece in (p0, p1, p2, p3)]
            parts = []
            for basis in range(7):
                value = [zero, zero]
                for r in range(4):
                    if 0 <= basis - r <= 4:
                        value = [jnp.where(at[basis - r], pieces[r][k], value[k]) for k in range(2)]
                parts.append(value)
            parts.append(split(0.5 * normed * (1.0 + jnp.tanh(0.5 * normed))))
            columns = []
            for z in range(4):
                columns.append(
                    jnp.concatenate(
                        [part[0][16 * z : 16 * z + 16] for part in parts]
                        + [part[1][16 * z : 16 * z + 16] for part in parts],
                        axis=0,
                    )
                )
            product = dot(weights, jnp.concatenate(columns, axis=1))
            for z in range(4):
                value = product[0:16, 128 * z : 128 * z + 128] + product[16:32, 128 * z : 128 * z + 128]
                result_ref[half, pl.ds(z * 16 + x, 16, stride=PITCH), :] = value + constant
            return carry

        for part in range(2):
            lax.fori_loop(8 * part, 8 * part + 8, step, 0, unroll=8)
            for z in range(4):
                row = 16 * z + 8 * part
                copy = pltpu.make_async_copy(
                    result_ref.at[half].reshape(16, PITCH, 128).at[:, row : row + 8, :],
                    out_ref.at[:, row : row + 8, lanes],
                    sems.at[8 * half + 4 * part + z],
                )
                copy.start()
                copies.append(copy)
    for copy in copies:
        copy.wait()


def whole():
    return pl.BlockSpec(memory_space=pltpu.VMEM)


def scalars():
    return pl.BlockSpec(memory_space=pltpu.SMEM)


def hbm():
    return pl.BlockSpec(memory_space=pltpu.HBM)


def params(vmem):
    return pltpu.CompilerParams(vmem_limit_bytes=vmem * MIB)


def cost(flops, moved):
    return pl.CostEstimate(flops=flops, bytes_accessed=moved, transcendentals=0)


def shape(dims, dtype=F32):
    return jax.ShapeDtypeStruct(dims, dtype)


def far(*arrays):
    return [pltpu.with_memory_space_constraint(array, pltpu.HBM) for array in arrays]


def near(*arrays):
    return [pltpu.with_memory_space_constraint(array, pltpu.VMEM) for array in arrays]


def transfers(count):
    return pltpu.SemaphoreType.DMA((count,))


def forward_call(field, weight):
    y_high, y_low = split_table(Y_FORWARD)
    return pl.pallas_call(
        forward_kernel,
        out_shape=(pltpu.VMEM((512, 128), F32), pltpu.VMEM((128, 128), F32), pltpu.VMEM((128, 128), F32)),
        in_specs=[hbm()] * 4,
        out_specs=(whole(),) * 3,
        scratch_shapes=[
            pltpu.SMEM((2, 512), F32),
            pltpu.VMEM((256, 128), F32),
            pltpu.VMEM((1024, 128), F32),
            pltpu.VMEM((2, 1024, 128), F32),
            pltpu.VMEM((1024, 32), F32),
            pltpu.VMEM((256, 256), B16),
            pltpu.VMEM((4, 256, 256), B16),
            transfers(5),
        ],
        compiler_params=params(24),
        cost_estimate=cost(4 * 10**8, 4 * 10**6),
        name="forward",
    )(
        *far(jnp.asarray(PHASE), field, weight, jnp.asarray(np.concatenate([y_high, y_low], axis=1)))
    )


def local_call(field, local_weight, base_weight, spline_coef, index, bn_gain, bn_shift):
    y_table = np.concatenate(split_table(Y_BACK), axis=0)
    return pl.pallas_call(
        local_kernel,
        out_shape=(
            pltpu.VMEM((256, 128), F32),
            pltpu.VMEM((128, 64), F32),
            pltpu.VMEM((16, 16), F32),
            pltpu.VMEM((1024, 256), F32), pltpu.VMEM((32, 128), F32), pltpu.VMEM((32, 256), B16), pltpu.VMEM((16, 128), F32),
            pltpu.VMEM((2, 16 * PITCH, 128), jnp.int32),
            pltpu.VMEM((64, 256), B16),
            pltpu.VMEM((16, 128), F32),
            pltpu.VMEM((16, 128), F32),
        ),
        in_specs=[hbm()] * 10,
        out_specs=(whole(),) * 11,
        scratch_shapes=[
            pltpu.VMEM((16, 16), F32),
            pltpu.VMEM((16, 8, 16), F32),
            pltpu.VMEM((2, 16 * PITCH, 128), F32),
            pltpu.VMEM((2, 16), F32),
            transfers(12),
        ],
        compiler_params=params(24),
        cost_estimate=cost(10**8, 2 * 10**6),
        name="local",
    )(*far(field.reshape(16, 64, 256), local_weight, base_weight, jnp.transpose(spline_coef, (0, 2, 1)), index.reshape(16, 64, 256),
            jnp.asarray(y_table), bn_gain.reshape(1, 16), bn_shift.reshape(1, 16),
            jnp.asarray(Z_FORWARD, F32), jnp.asarray(Z_BACK, F32)))


def mix_call(got, partner, kept, z_forward, z_back, local_weight, stat, weight):
    return pl.pallas_call(
        mix_kernel,
        out_shape=pltpu.VMEM((768, 128), F32),
        in_specs=[whole()] * 7 + [hbm()] * 2,
        out_specs=whole(),
        scratch_shapes=[
            pltpu.SMEM((2, 512), F32),
            pltpu.VMEM((128, 128), F32),
            pltpu.VMEM((1024, 32), F32),
            pltpu.VMEM((256, 128), F32),
            transfers(2),
        ],
        compiler_params=params(24),
        cost_estimate=cost(10**7, 10**6),
        name="mix",
    )(*near(got, partner, kept, z_forward, z_back, local_weight, stat), *far(jnp.asarray(PHASE), weight))


def output_call(back, hidden, kan, constant, index, y_table, gain, bias):
    return pl.pallas_call(
        output_kernel,
        out_shape=pltpu.HBM((16, 64, 256), F32),
        in_specs=[whole()] * 8,
        out_specs=hbm(),
        scratch_shapes=[
            pltpu.VMEM((4, 128, 256), B16),
            pltpu.VMEM((4, 128, 256), B16),
            pltpu.VMEM((1024, 256), F32),
            pltpu.VMEM((2, 16 * PITCH, 128), F32),
            transfers(16),
        ],
        compiler_params=params(24),
        cost_estimate=cost(10**9, 6 * 10**6),
        name="output",
    )(*near(back, hidden, kan, constant, index, y_table, gain, bias))


def on_device(
    field, spline_index, spec_weight, local_weight, bn_gain, bn_shift, base_weight, spline_coef
):
    field = field.reshape(1024, 256)
    index = spline_index.reshape(1024, 256)
    weight = jnp.transpose(spec_weight, (0, 1, 2, 4, 5, 3)).reshape(1024, 32)
    sent, own, kept = forward_call(field, weight)
    path = [0]
    while path[-1] != 8:
        path.append(15 - path[-1] if path[-1] < 8 else 16 - path[-1])
    partner = lax.ppermute(own, BOTH, [(16 * a, 16 * b) for a, b in zip(path[:-1], path[1:])])
    got = lax.all_to_all(sent.reshape(256, 2, 128), BOTH, 0, 0, tiled=True).reshape(512, 128)
    z_forward, z_back, maps, hidden, stat, *rest = local_call(
        field, local_weight, base_weight, spline_coef, index, bn_gain, bn_shift
    )
    back = mix_call(got, partner, kept, z_forward, z_back, maps, stat, weight)
    back = lax.all_to_all(back.reshape(256, 1, 384), BOTH, 0, 0, tiled=True).reshape(768, 128)
    output = output_call(back, hidden, *rest)
    return output.reshape(16, 4, 16, 256)


def solution(mesh):
    in_specs = (
        P(None, "pa", "pb", None),
        P(None, "pa", "pb", None),
        P(None, None, None, None, "pa", "pb"),
        P(),
        P(),
        P(),
        P(),
        P(),
    )
    out_specs = P(None, "pa", "pb", None)
    return jax.shard_map(
        on_device, mesh=mesh, in_specs=in_specs, out_specs=out_specs, check_vma=False
    )
```

```python
import jax
import jax.numpy as jnp
import numpy as np
from jax import lax
from jax.experimental import pallas as pl
from jax.experimental.pallas import tpu as pltpu
from jax.sharding import PartitionSpec as P

NZ, NX, NY = 64, 256, 256
CELLS = NZ * NX * NY
BLOCK_CELLS = 4 * 16 * 256
EPSILON = 1e-05
EXACT = lax.Precision.HIGHEST
F32 = jnp.float32
B16 = jnp.bfloat16
BOTH = ("pa", "pb")
MIB = 1024 * 1024
PITCH = 72

KZ = np.array([j if j < 16 else j - 32 for j in range(32)])
KY = np.arange(16)


def split_table(table):
    high = jnp.asarray(table, F32).astype(B16)
    high = np.asarray(table, np.float32).astype(jnp.bfloat16)
    low = (np.asarray(table, np.float64) - high.astype(np.float64)).astype(jnp.bfloat16)
    return high, low


def rotation(angle, sign):
    cosine, sine = np.cos(angle), np.sin(angle)
    return np.stack([np.stack([cosine, -sign * sine]), np.stack([sign * sine, cosine])])


def tables():
    angle = 2 * np.pi * (np.arange(NY)[:, None] * KY % NY) / NY
    y_part = np.stack([np.cos(angle), -np.sin(angle)], axis=1)
    y_forward = np.tile(y_part.reshape(NY, 32), (1, 4))
    weight = np.where(KY == 0, 1.0, 2.0) / CELLS
    y_back = np.einsum("ypk,k->pky", y_part, weight).reshape(32, NY)
    z = 4 * np.arange(16)[None, :] + np.arange(4)[:, None]
    angle = 2 * np.pi * (z[:, :, None] * KZ % NZ) / NZ
    z_forward = np.einsum("qpzaj,hH->pzhaqHj", rotation(angle, -1.0), np.eye(2)).reshape(256, 128)
    angle = 2 * np.pi * (z[:, :, None] * KZ % NZ) / NZ
    z_back = np.einsum("qpzaj->qzapj", rotation(angle, 1.0)).reshape(128, 64)
    return y_forward, y_back, z_forward, z_back


Y_FORWARD, Y_BACK, Z_FORWARD, Z_BACK = tables()
PHASE = np.stack([np.cos(2 * np.pi * np.arange(512) / 512), np.sin(2 * np.pi * np.arange(512) / 512)]).astype(np.float32)


def split(values):
    high = values.astype(B16)
    return high, (values - high.astype(F32)).astype(B16)


def dot(left, right):
    return jnp.dot(left, right, preferred_element_type=F32)


def dot_nt(left, right, precision=None):
    return lax.dot_general(left, right, (((1,), (1,)), ((), ())), precision=precision, preferred_element_type=F32)


def dot_exact(left, right):
    return jnp.dot(left, right, precision=EXACT, preferred_element_type=F32)


def iota(shape, axis):
    return lax.broadcasted_iota(jnp.int32, shape, axis)


def phase_index(frequency, block):
    return (frequency * (32 * block + 15)) & 511


def place(frequency):
    return (frequency % 32) // 2, frequency % 2


def cosine(frequency, step):
    return float(np.cos(2 * np.pi * frequency * (step + 0.5) / NX))


def sine(frequency, step):
    return float(np.sin(2 * np.pi * frequency * (step + 0.5) / NX))


def signs(rows, first):
    return jnp.where(iota((rows, 128), 1) < 64, first, -first).astype(F32)


def forward_kernel(
    phase_hbm, field_hbm, weight_hbm, y_hbm, out_ref, sent_ref, kept_ref,
    phase_ref, half_ref, rows_ref, field_ref, weight_ref, small_ref, y_ref, sems,
):
    pa, pb = lax.axis_index("pa"), lax.axis_index("pb")
    copies = [
        pltpu.make_async_copy(source, target, sems.at[number])
        for number, (source, target) in enumerate(
            [
                (y_hbm, small_ref),
                (field_hbm.at[:, 0:128], field_ref.at[0]),
                (field_hbm.at[:, 128:256], field_ref.at[1]),
                (weight_hbm, weight_ref),
                (phase_hbm, phase_ref),
            ]
        )
    ]
    for copy in copies:
        copy.start()
    copies[0].wait()
    small = small_ref[...].reshape(16, 16, 256)
    for xj in range(4):
        mine = (iota((16, 256), 1) % 128 // 32 == xj).astype(F32).astype(B16)
        y_ref[xj] = (small * mine[None]).reshape(256, 256)
    for copy in copies[1:3]:
        copy.wait()
    total = jnp.zeros((256, 128), F32)
    for xj in range(4):
        piece = jnp.concatenate(
            [field_ref[half, pl.ds(xj, 256, stride=4), :] for half in range(2)], axis=1
        )
        high, low = split(piece)
        product = dot(high, y_ref[xj])
        total = total + product[:, 0:128] + product[:, 128:256] + dot(low, y_ref[xj, :, 0:128])
    half_ref[...] = total
    copies[4].wait()
    lines = []
    for x4 in range(4):
        piece = jnp.concatenate([half_ref[pl.ds(z * 4 + x4, 16, stride=16), :] for z in range(4)], axis=0).T
        for xj in range(4):
            lines.append(jnp.concatenate([piece[32 * xj : 32 * xj + 16], piece[32 * xj + 16 : 32 * xj + 32]], axis=1))
    sign = signs(8, 1.0)
    for half in range(2):
        rows = slice(8 * half, 8 * half + 8)
        even = [lines[8 + j][rows] + lines[7 - j][rows] for j in range(8)]
        odd = [pltpu.roll(lines[8 + j][rows] - lines[7 - j][rows], 64, axis=1) * sign for j in range(8)]
        for frequency in range(17):
            first = sum(even[j] * cosine(frequency, j) for j in range(8))
            second = sum(odd[j] * sine(frequency, j) for j in range(8))
            values = {}
            if frequency < 16:
                values[frequency] = first + second
            if frequency > 0:
                values[-frequency] = first - second
            for signed, value in values.items():
                index = phase_index(signed, pb)
                kxp, kxl = place(signed)
                out_ref[pl.ds(kxp * 32 + kxl + 16 * half, 8, stride=2), :] = value * phase_ref[0, index] + pltpu.roll(
                    value, 64, axis=1
                ) * (sign * phase_ref[1, index])
    copies[3].wait()

    @pl.when(pb == 0)
    def _():
        rows_ref[:, 0:32] = weight_ref[...]
        for target, wanted in ((sent_ref, jnp.where(pa < 8, 1, 0)), (kept_ref, 0)):
            chosen = rows_ref[pl.ds(wanted, 512, stride=2), :]
            target[...] = jnp.concatenate([chosen[128 * q : 128 * (q + 1), 0:32] for q in range(4)], axis=1)


def local_kernel(
    field_hbm, map_hbm, base_hbm, coef_hbm, index_hbm, y_hbm, gain_hbm, bias_hbm, z_hbm, back_hbm,
    z_ref, back_ref, map_ref, hidden_ref, stat_ref, kan_ref, shift_ref, index_ref, y_ref, gain_ref, bias_ref,
    base_ref, coef_ref, field_ref, row_ref, sems,
):
    copies = [
        pltpu.make_async_copy(
            field_hbm.at[:, :, 128 * half : 128 * half + 128],
            field_ref.at[half].reshape(16, PITCH, 128).at[:, 0:64, :],
            sems.at[half],
        )
        for half in range(2)
    ]
    small = [
        pltpu.make_async_copy(source, target, sems.at[2 + number])
        for number, (source, target) in enumerate([(map_hbm, map_ref), (base_hbm, base_ref), (coef_hbm, coef_ref)])
    ] + [
        pltpu.make_async_copy(gain_hbm, row_ref.at[0:1, :], sems.at[8]),
        pltpu.make_async_copy(bias_hbm, row_ref.at[1:2, :], sems.at[9]),
    ]
    moved = [
        pltpu.make_async_copy(y_hbm, y_ref, sems.at[7]),
        pltpu.make_async_copy(z_hbm, z_ref, sems.at[10]),
        pltpu.make_async_copy(back_hbm, back_ref, sems.at[11]),
    ] + [
        pltpu.make_async_copy(
            index_hbm.at[:, :, 128 * half : 128 * half + 128],
            index_ref.at[half].reshape(16, PITCH, 128).at[:, 0:64, :],
            sems.at[5 + half],
        )
        for half in range(2)
    ]
    for copy in small + copies + moved:
        copy.start()
    for copy in small:
        copy.wait()
    last = coef_ref[:, 7, :]
    pieces = [coef_ref[:, basis, :] - last for basis in range(7)] + [base_ref[...]]
    high, low = split(jnp.concatenate(pieces, axis=1))
    kan_ref[0:16, 0:128] = high
    kan_ref[0:16, 128:256] = high
    kan_ref[16:32, 0:128] = low
    kan_ref[16:32, 128:256] = jnp.zeros((16, 128), B16)
    shift_ref[...] = jnp.broadcast_to(jnp.sum(last, axis=1, keepdims=True), (16, 128))
    gain_ref[...] = jnp.broadcast_to(column(row_ref[0:1, :]), (16, 128))
    bias_ref[...] = jnp.broadcast_to(column(row_ref[1:2, :]), (16, 128))
    high, low = split(map_ref[...])
    zero = jnp.zeros((16, 16), B16)
    maps = jnp.concatenate(
        [jnp.concatenate([high, high], axis=1), jnp.concatenate([low, zero], axis=1)], axis=0
    )
    for copy in copies:
        copy.wait()

    def step(x, total):
        for z in range(4):
            rows = pl.ds(z * 16 + x, 16, stride=PITCH)
            high, low = split(jnp.concatenate([field_ref[half, rows, :] for half in range(2)], axis=1))
            both = dot(maps, jnp.concatenate([high, low], axis=0))
            value = both[0:16] + both[16:32]
            total = total + value
            start = pl.multiple_of(x * 64 + z * 16, 16)
            hidden_ref[pl.ds(start, 16), :] = value
        return total

    total = lax.fori_loop(0, 16, step, jnp.zeros((16, 256), F32), unroll=4)
    mean = jnp.sum(total, axis=1, keepdims=True) * (1.0 / BLOCK_CELLS)

    def spread(part, total):
        for z in range(4):
            start = pl.multiple_of(part * 64 + z * 16, 16)
            away = hidden_ref[pl.ds(start, 16), :] - mean
            total = total + away * away
        return total

    total = lax.fori_loop(0, 16, spread, jnp.zeros((16, 256), F32), unroll=4)
    squares = jnp.sum(total, axis=1, keepdims=True)
    first = iota((16, 128), 1) == 0
    stat_ref[0:16, :] = jnp.where(first, mean, 0.0)
    stat_ref[16:32, :] = jnp.where(first, squares, 0.0)
    for copy in moved:
        copy.wait()


def mix_kernel(
    got_ref, partner_ref, kept_ref, z_ref, back_ref, map_ref, stat_ref, phase_hbm, weight_hbm, out_ref,
    phase_ref, rows_ref, weight_ref, both_ref, sems,
):
    pa, pb = lax.axis_index("pa"), lax.axis_index("pb")
    copies = [
        pltpu.make_async_copy(source, target, sems.at[number])
        for number, (source, target) in enumerate(
            [
                (weight_hbm, weight_ref),
                (phase_hbm, phase_ref),
            ]
        )
    ]
    for copy in copies:
        copy.start()
    total = jnp.sum(got_ref[...].reshape(16, 4, 8, 128), axis=1)
    total = total + pltpu.roll(total, 4, axis=1)
    total = total + pltpu.roll(total, 2, axis=1)
    rows_ref[...] = total.reshape(128, 128)
    lines = jnp.concatenate([rows_ref[pl.ds(0, 16, stride=8), :], rows_ref[pl.ds(1, 16, stride=8), :]], axis=0)
    lines = lines.T
    lines = jnp.concatenate([lines[16 * q : 16 * (q + 1)] for q in range(8)], axis=1)
    modes = dot_exact(lines, z_ref[...])
    real = [modes[:, 32 * k : 32 * k + 32] for k in range(2)]
    imag = [modes[:, 64 + 32 * k : 96 + 32 * k] for k in range(2)]
    lower = pa < 8
    far_real = jnp.where(lower, real[0], real[1])
    far_imag = jnp.where(lower, imag[0], imag[1])
    odd = iota((32, 32), 0) % 2 == 1
    twice = (iota((32, 16), 0) // 2 == iota((32, 16), 1)).astype(F32)
    map_rows = dot_exact(twice, map_ref[...])
    mixed_real = jnp.zeros((32, 32), F32)
    mixed_imag = jnp.zeros((32, 32), F32)
    local_real = jnp.zeros((32, 32), F32)
    local_imag = jnp.zeros((32, 32), F32)
    partner_real = jnp.zeros((32, 32), F32)
    partner_imag = jnp.zeros((32, 32), F32)
    copies[0].wait()
    source, target = iota((128, 128), 0), iota((128, 128), 1)
    turn = jnp.logical_and(source // 32 == target // 32, source % 32 == (32 - target % 32) % 32)
    turn = jnp.logical_and(turn, target % 32 != 16).astype(F32)
    turned = dot_exact(jnp.where(pa == 0, kept_ref[...], partner_ref[...]), turn)
    both_ref[pl.ds(0, 128, stride=2), :] = turned
    both_ref[pl.ds(1, 128, stride=2), :] = turned
    for i in range(16):
        mode_real = jnp.where(odd, real[1][i : i + 1], real[0][i : i + 1])
        mode_imag = jnp.where(odd, imag[1][i : i + 1], imag[0][i : i + 1])
        weight_real = weight_ref[32 * i : 32 * i + 32, :]
        weight_imag = weight_ref[512 + 32 * i : 544 + 32 * i, :]
        mixed_real = mixed_real + weight_real * mode_real - weight_imag * mode_imag
        mixed_imag = mixed_imag + weight_real * mode_imag + weight_imag * mode_real
        column = map_rows[:, i : i + 1]
        local_real = local_real + column * mode_real
        local_imag = local_imag + column * mode_imag
        row = 32 * (i % 8)
        lane = 32 * (i // 8)
        weight_real = both_ref[row : row + 32, lane : lane + 32]
        weight_imag = both_ref[row : row + 32, 64 + lane : 96 + lane]
        mode_real = far_real[i : i + 1]
        mode_imag = far_imag[i : i + 1]
        partner_real = partner_real + weight_real * mode_real + weight_imag * mode_imag
        partner_imag = partner_imag + weight_imag * mode_real - weight_real * mode_imag
    origin = jnp.logical_and(
        jnp.logical_and(pa == 0, pb == 0), jnp.logical_and(iota((32, 32), 0) % 2 == 0, iota((32, 32), 1) == 0)
    )
    centre = jnp.where(origin, mixed_real, 0.0)
    moved_real = jnp.where(origin, 0.0, mixed_real)
    moved_imag = jnp.where(origin, 0.0, mixed_imag)
    own = jnp.where(pb == 0, 0.5, 2.0)
    cross = jnp.where(pb == 0, 2.0, 4.0)
    power = own * (moved_real * moved_real + moved_imag * moved_imag)
    power = power + cross * (moved_real * local_real + moved_imag * local_imag)
    pair = moved_real * partner_real - moved_imag * partner_imag
    chosen = jnp.where(lower, 0, 1)
    pair = jnp.where(
        jnp.logical_and(pb == 0, iota((32, 32), 0) % 2 == chosen), jnp.where(pa == 0, 0.5, 1.0) * pair, 0.0
    )
    power = power + pair
    sums = jnp.concatenate(
        [
            power * (1.0 / CELLS),
            jnp.zeros((16, 32), F32),
            stat_ref[:, 0:32],
            centre * (1.0 / CELLS),
            jnp.zeros((16, 32), F32),
        ],
        axis=0,
    )
    sums = dot_nt(jnp.ones((8, 32), F32), sums, EXACT)
    out_ref[pl.ds(2, 256, stride=3), :] = jnp.broadcast_to(sums[0:1], (256, 128))
    order = (iota((32, 32), 1) == 2 * (iota((32, 32), 0) % 16) + iota((32, 32), 0) // 16).astype(F32)
    mixed = dot_exact(order, jnp.concatenate([mixed_real, mixed_imag], axis=1))
    copies[1].wait()
    planes = dot_nt(back_ref[...], mixed, EXACT)
    sign = signs(16, -1.0)
    for kxl in range(2):
        frequency = 2 * pa + kxl - jnp.where(lower, 0, 32)
        value = jnp.concatenate(
            [planes[16 * q : 16 * (q + 1), 16 * kxl : 16 * kxl + 16] for q in range(8)], axis=1
        )
        other = pltpu.roll(value, 64, axis=1) * sign
        for block in range(16):
            index = phase_index(frequency, block)
            out_ref[pl.ds(block * 3 + kxl, 16, stride=48), :] = (
                value * phase_ref[0, index] + other * phase_ref[1, index]
            )


def column(row):
    eye = (iota((16, 16), 0) == iota((16, 16), 1)).astype(F32)
    return dot_nt(eye, jnp.broadcast_to(row, (8, 16)), EXACT)[:, 0:1]


def output_kernel(
    got_ref, hidden_ref, kan_ref, constant_ref, index_ref, small_ref, gain_ref, bias_ref, out_ref,
    y_high_ref, y_low_ref, spec_ref, result_ref, sems,
):
    stats = got_ref[pl.ds(2, 256, stride=3), :]
    sums = jnp.sum(stats, axis=0, keepdims=True)
    mean = sums * (1.0 / 256)
    away = stats - mean
    between = jnp.sum(away * away, axis=0, keepdims=True) * float(BLOCK_CELLS)
    lane = iota((1, 128), 1)
    is_mean = jnp.logical_and(lane >= 48, lane < 64)
    is_centre = jnp.logical_and(lane >= 80, lane < 112)
    variance = jnp.where(is_mean, between, jnp.where(lane < 80, sums, 0.0)) * (1.0 / CELLS)
    mean = jnp.where(is_mean, mean, jnp.where(is_centre, sums, 0.0))
    lane, row = iota((16, 128), 1), iota((16, 128), 0)
    owner = jnp.where(
        lane < 32, lane // 2, jnp.where(lane < 80, lane % 16, jnp.where(lane < 112, (lane - 80) // 2, -1))
    )
    pick = (owner == row).astype(F32)
    mean = dot_nt(pick, jnp.broadcast_to(mean, (8, 128)), EXACT)[:, 0:1]
    variance = dot_nt(pick, jnp.broadcast_to(variance, (8, 128)), EXACT)[:, 0:1]
    scale = gain_ref[:, 0:1] * lax.rsqrt(jnp.maximum(variance, 0.0) + EPSILON)
    mean = jnp.broadcast_to(jnp.concatenate([mean] * 4, axis=0), (64, 128))
    scale = jnp.broadcast_to(jnp.concatenate([scale] * 4, axis=0), (64, 128))
    bias = jnp.broadcast_to(jnp.concatenate([bias_ref[:, 0:1]] * 4, axis=0), (64, 128))
    lines = [[None] * 2 for _ in range(16)]
    sign = signs(8, -1.0)
    for half in range(2):
        modes = {}
        for frequency in range(-16, 16):
            kxp, kxl = place(frequency)
            modes[frequency] = got_ref[pl.ds(kxp * 48 + kxl + 24 * half, 8, stride=3), :]
        even = [modes[k] + modes[-k] for k in range(1, 16)] + [modes[-16]]
        odd = [modes[k] - modes[-k] for k in range(1, 16)] + [-modes[-16]]
        odd = [pltpu.roll(value, 64, axis=1) * sign for value in odd]
        for j in range(8):
            first = modes[0] + sum(even[k - 1] * cosine(k, j) for k in range(1, 17))
            second = sum(odd[k - 1] * sine(k, j) for k in range(1, 17))
            lines[8 + j][half] = first + second
            lines[7 - j][half] = first - second
    groups = []
    for x4 in range(4):
        piece = jnp.concatenate([lines[4 * x4 + xj][half] for xj in range(4) for half in range(2)], axis=0).T
        groups.append(jnp.concatenate([piece[0:64], piece[64:128]], axis=1))
    high, low = split(jnp.concatenate(groups, axis=0))
    both = jnp.concatenate([high, low], axis=0)
    for number, table in enumerate((y_high_ref, y_low_ref)):
        table[...] = jnp.zeros((4, 128, 256), B16)
        for xj in range(4):
            for part in range(2):
                start = 32 * number + 16 * part
                row = 64 * part + 16 * xj
                table[xj, row : row + 16, :] = small_ref[start : start + 16, :]
    for xj in range(4):
        product = dot(both, y_high_ref[xj])
        value = product[0:256] + product[256:512] + dot(high, y_low_ref[xj])
        for x4 in range(4):
            start = (4 * x4 + xj) * 64
            spec_ref[start : start + 64, :] = value[64 * x4 : 64 * x4 + 64]
    weights = kan_ref[...]
    constant = constant_ref[...]
    copies = []
    for half in range(2):
        lanes = slice(128 * half, 128 * half + 128)

        def step(x, carry, half=half, lanes=lanes):
            rows = pl.ds(pl.multiple_of(x * 64, 64), 64)
            hidden = spec_ref[rows, lanes] + hidden_ref[rows, lanes]
            normed = (hidden - mean) * scale + bias
            level = jnp.concatenate(
                [index_ref[half, pl.ds(z * 16 + x, 16, stride=PITCH), :] for z in range(4)], axis=0
            ).astype(F32)
            local = jnp.clip(normed * 1.25 + (2.5 - level), 0.0, 1.0)
            other = 1.0 - local
            square = local * local
            cube = square * local
            p0 = other * other * other * (1.0 / 6.0)
            p3 = cube * (1.0 / 6.0)
            p1 = 0.5 * cube - square + 2.0 / 3.0
            p2 = 0.5 * (square + local - cube) + 1.0 / 6.0
            level = level.astype(B16)
            at = [level == jnp.asarray(k, B16) for k in range(5)]
            zero = jnp.zeros((64, 128), B16)
            pieces = [split(piece) for piece in (p0, p1, p2, p3)]
            parts = []
            for basis in range(7):
                value = [zero, zero]
                for r in range(4):
                    if 0 <= basis - r <= 4:
                        value = [jnp.where(at[basis - r], pieces[r][k], value[k]) for k in range(2)]
                parts.append(value)
            parts.append(split(0.5 * normed * (1.0 + jnp.tanh(0.5 * normed))))
            columns = []
            for z in range(4):
                columns.append(
                    jnp.concatenate(
                        [part[0][16 * z : 16 * z + 16] for part in parts]
                        + [part[1][16 * z : 16 * z + 16] for part in parts],
                        axis=0,
                    )
                )
            product = dot(weights, jnp.concatenate(columns, axis=1))
            for z in range(4):
                value = product[0:16, 128 * z : 128 * z + 128] + product[16:32, 128 * z : 128 * z + 128]
                result_ref[half, pl.ds(z * 16 + x, 16, stride=PITCH), :] = value + constant
            return carry

        for part in range(2):
            lax.fori_loop(8 * part, 8 * part + 8, step, 0, unroll=8)
            for z in range(4):
                row = 16 * z + 8 * part
                copy = pltpu.make_async_copy(
                    result_ref.at[half].reshape(16, PITCH, 128).at[:, row : row + 8, :],
                    out_ref.at[:, row : row + 8, lanes],
                    sems.at[8 * half + 4 * part + z],
                )
                copy.start()
                copies.append(copy)
    for copy in copies:
        copy.wait()


def whole():
    return pl.BlockSpec(memory_space=pltpu.VMEM)


def scalars():
    return pl.BlockSpec(memory_space=pltpu.SMEM)


def hbm():
    return pl.BlockSpec(memory_space=pltpu.HBM)


def params(vmem):
    return pltpu.CompilerParams(vmem_limit_bytes=vmem * MIB)


def cost(flops, moved):
    return pl.CostEstimate(flops=flops, bytes_accessed=moved, transcendentals=0)


def shape(dims, dtype=F32):
    return jax.ShapeDtypeStruct(dims, dtype)


def far(*arrays):
    return [pltpu.with_memory_space_constraint(array, pltpu.HBM) for array in arrays]


def near(*arrays):
    return [pltpu.with_memory_space_constraint(array, pltpu.VMEM) for array in arrays]


def transfers(count):
    return pltpu.SemaphoreType.DMA((count,))


def forward_call(field, weight):
    y_high, y_low = split_table(Y_FORWARD)
    return pl.pallas_call(
        forward_kernel,
        out_shape=(pltpu.VMEM((512, 128), F32), pltpu.VMEM((128, 128), F32), pltpu.VMEM((128, 128), F32)),
        in_specs=[hbm()] * 4,
        out_specs=(whole(),) * 3,
        scratch_shapes=[
            pltpu.SMEM((2, 512), F32),
            pltpu.VMEM((256, 128), F32),
            pltpu.VMEM((1024, 128), F32),
            pltpu.VMEM((2, 1024, 128), F32),
            pltpu.VMEM((1024, 32), F32),
            pltpu.VMEM((256, 256), B16),
            pltpu.VMEM((4, 256, 256), B16),
            transfers(5),
        ],
        compiler_params=params(24),
        cost_estimate=cost(4 * 10**8, 4 * 10**6),
        name="forward",
    )(
        *far(jnp.asarray(PHASE), field, weight, jnp.asarray(np.concatenate([y_high, y_low], axis=1)))
    )


def local_call(field, local_weight, base_weight, spline_coef, index, bn_gain, bn_shift):
    y_table = np.concatenate(split_table(Y_BACK), axis=0)
    return pl.pallas_call(
        local_kernel,
        out_shape=(
            pltpu.VMEM((256, 128), F32),
            pltpu.VMEM((128, 64), F32),
            pltpu.VMEM((16, 16), F32),
            pltpu.VMEM((1024, 256), F32), pltpu.VMEM((32, 128), F32), pltpu.VMEM((32, 256), B16), pltpu.VMEM((16, 128), F32),
            pltpu.VMEM((2, 16 * PITCH, 128), jnp.int32),
            pltpu.VMEM((64, 256), B16),
            pltpu.VMEM((16, 128), F32),
            pltpu.VMEM((16, 128), F32),
        ),
        in_specs=[hbm()] * 10,
        out_specs=(whole(),) * 11,
        scratch_shapes=[
            pltpu.VMEM((16, 16), F32),
            pltpu.VMEM((16, 8, 16), F32),
            pltpu.VMEM((2, 16 * PITCH, 128), F32),
            pltpu.VMEM((2, 16), F32),
            transfers(12),
        ],
        compiler_params=params(24),
        cost_estimate=cost(10**8, 2 * 10**6),
        name="local",
    )(*far(field.reshape(16, 64, 256), local_weight, base_weight, jnp.transpose(spline_coef, (0, 2, 1)), index.reshape(16, 64, 256),
            jnp.asarray(y_table), bn_gain.reshape(1, 16), bn_shift.reshape(1, 16),
            jnp.asarray(Z_FORWARD, F32), jnp.asarray(Z_BACK, F32)))


def mix_call(got, partner, kept, z_forward, z_back, local_weight, stat, weight):
    return pl.pallas_call(
        mix_kernel,
        out_shape=pltpu.VMEM((768, 128), F32),
        in_specs=[whole()] * 7 + [hbm()] * 2,
        out_specs=whole(),
        scratch_shapes=[
            pltpu.SMEM((2, 512), F32),
            pltpu.VMEM((128, 128), F32),
            pltpu.VMEM((1024, 32), F32),
            pltpu.VMEM((256, 128), F32),
            transfers(2),
        ],
        compiler_params=params(24),
        cost_estimate=cost(10**7, 10**6),
        name="mix",
    )(*near(got, partner, kept, z_forward, z_back, local_weight, stat), *far(jnp.asarray(PHASE), weight))


def output_call(back, hidden, kan, constant, index, y_table, gain, bias):
    return pl.pallas_call(
        output_kernel,
        out_shape=pltpu.HBM((16, 64, 256), F32),
        in_specs=[whole()] * 8,
        out_specs=hbm(),
        scratch_shapes=[
            pltpu.VMEM((4, 128, 256), B16),
            pltpu.VMEM((4, 128, 256), B16),
            pltpu.VMEM((1024, 256), F32),
            pltpu.VMEM((2, 16 * PITCH, 128), F32),
            transfers(16),
        ],
        compiler_params=params(24),
        cost_estimate=cost(10**9, 6 * 10**6),
        name="output",
    )(*near(back, hidden, kan, constant, index, y_table, gain, bias))


def on_device(
    field, spline_index, spec_weight, local_weight, bn_gain, bn_shift, base_weight, spline_coef
):
    field = field.reshape(1024, 256)
    index = spline_index.reshape(1024, 256)
    weight = jnp.transpose(spec_weight, (0, 1, 2, 4, 5, 3)).reshape(1024, 32)
    sent, own, kept = forward_call(field, weight)
    path = [0]
    while path[-1] != 8:
        path.append(15 - path[-1] if path[-1] < 8 else 16 - path[-1])
    partner = lax.ppermute(own, BOTH, [(16 * a, 16 * b) for a, b in zip(path[:-1], path[1:])])
    got = lax.all_to_all(sent.reshape(256, 2, 128), BOTH, 0, 0, tiled=True).reshape(512, 128)
    z_forward, z_back, maps, hidden, stat, *rest = local_call(
        field, local_weight, base_weight, spline_coef, index, bn_gain, bn_shift
    )
    back = mix_call(got, partner, kept, z_forward, z_back, maps, stat, weight)
    back = lax.all_to_all(back.reshape(256, 1, 384), BOTH, 0, 0, tiled=True).reshape(768, 128)
    output = output_call(back, hidden, *rest)
    return output.reshape(16, 4, 16, 256)


def solution(mesh):
    in_specs = (
        P(None, "pa", "pb", None),
        P(None, "pa", "pb", None),
        P(None, None, None, None, "pa", "pb"),
        P(),
        P(),
        P(),
        P(),
        P(),
    )
    out_specs = P(None, "pa", "pb", None)
    return jax.shard_map(
        on_device, mesh=mesh, in_specs=in_specs, out_specs=out_specs, check_vma=False
    )
```
